128 devices in a mesh: node: 16 (over y, z), local: 8 (over x, core).
Axes of the slice: x: 4, y: 4, z: 4, core: 2. Of those that a mesh axis runs over, the one named last changes fastest.
Arguments:
- tokens: bfloat16 [16384, 2048], P(('node', 'local')), may hold values from -6 to 6
- grad_out: bfloat16 [16384, 2048], P(('node', 'local')), may hold values from -6 to 6
- gate_weights: float32 [16384, 2], P(('node', 'local')), may hold values from 0.2 to 1
- expert_ids: int32 [16384, 2], P(('node', 'local')), may hold values from 0 to 7, as said below
- slot_ids: int32 [16384, 2], P(('node', 'local')), may hold values from 0 to 16, as said below
- counts: int32 [128, 8], P(('node', 'local')), may hold values from 0 to 16, as said below
- w_in: bfloat16 [8, 2048, 8192], P('local', None, 'node'), may hold values from -0.125 to 0.125
- w_out: bfloat16 [8, 8192, 2048], P('local', 'node'), may hold values from -0.0625 to 0.0625
Outputs:
- grad_tokens: bfloat16 [16384, 2048], P(('node', 'local'))
- grad_w_in: float32 [8, 2048, 8192], P('local', None, 'node')
- grad_w_out: float32 [8, 8192, 2048], P('local', 'node')
The draws below stay inside these ranges and needn't reach their ends.
Inputs may be any that keep to these rules, and one draw needn't show every extreme that they name: `expert_ids`: a token's two experts differ. slot_ids[t, k] is the number of earlier choices (in order of token, then k) on the same device naming the same expert, capped at 16. counts[d, e] is the number of choices on device d naming expert e, capped at 16.
All inputs are finite; a program needn't handle non-finite values.
Results may differ from the reference program's by a relative error of at most 0.0064.
Values may be sent and summed in bfloat16 or wider, within the bound.
A program may use at most 192 MiB of HBM per device.

```python
import jax
import jax.numpy as jnp
from jax import lax

D = 2048
FF = 8192
TOK_DEV = 128
EXPERTS = 8
CAP = 16
TOKENS = 16384
N_NODE = 16
N_LOCAL = 8


def routing(key):
    blocks = TOKENS // TOK_DEV
    key_first, key_offset, key_forced, key_light, key_quota, key_free, key_rest = jax.random.split(key, 7)
    position = jnp.arange(TOKENS) % TOK_DEV
    block_of = jnp.arange(TOKENS) // TOK_DEV
    forced = jax.random.randint(key_forced, (blocks,), 0, EXPERTS)
    light = (forced + jax.random.randint(key_light, (blocks,), 1, EXPERTS)) % EXPERTS
    quota = jax.random.randint(key_quota, (blocks,), 0, CAP)
    light_tok = light[block_of]
    is_open = position < quota[block_of]
    open_first = jax.random.randint(key_first, (TOKENS,), 0, EXPERTS)
    shut_first = (light_tok + 1 + jax.random.randint(key_rest, (TOKENS,), 0, EXPERTS - 1)) % EXPERTS
    first = jnp.where(is_open, open_first, shut_first)
    first = jnp.where(position <= CAP, forced[block_of], first)
    open_second = (first + jax.random.randint(key_offset, (TOKENS,), 1, EXPERTS)) % EXPERTS
    step = jax.random.randint(key_free, (TOKENS,), 0, EXPERTS - 2)
    distance = (light_tok - first) % EXPERTS
    shut_second = jnp.where(1 + step >= distance, first + 2 + step, first + 1 + step) % EXPERTS
    second = jnp.where(is_open, open_second, shut_second)
    chosen = jnp.stack([first, second], axis=1).astype(jnp.int32)
    flat_chosen = chosen.reshape(blocks, 2 * TOK_DEV)
    onehot = (flat_chosen[:, :, None] == jnp.arange(EXPERTS)[None, None, :]).astype(jnp.int32)
    earlier = jnp.cumsum(onehot, axis=1) - onehot
    ranks = jnp.sum(earlier * onehot, axis=2)
    slots = jnp.minimum(ranks, CAP).reshape(TOKENS, 2).astype(jnp.int32)
    filled = jnp.minimum(jnp.sum(onehot, axis=1), CAP).astype(jnp.int32)
    return (chosen, slots, filled)


def draw_expert_ids(key, part):
    return routing(key)[0]


def draw_slot_ids(key, part):
    return routing(key)[1]


def draw_counts(key, part):
    return routing(key)[2]


def levels(stream_key, dims, shards, low, top_value):
    loudness = 1.0
    for dim, blocks in shards:
        draws = jax.random.uniform(jax.random.fold_in(jax.random.fold_in(stream_key, 6), dim), (blocks,), jnp.float32, low / len(shards), top_value / len(shards))
        loudness = loudness * jnp.repeat(jnp.exp(draws), dims[dim] // blocks).reshape((-1,) + (1,) * (len(dims) - 1 - dim))
    return loudness


def normal_values(rng, dims, deviation, reach, cuts=(), held_as=jnp.bfloat16):
    values = deviation * jax.random.normal(rng, dims, jnp.float32)
    if cuts:
        values = values * levels(rng, dims, cuts, -0.22, 0.18)
    return jnp.clip(values, -reach, reach).astype(held_as)


def setup_inputs(seed: int = 0) -> dict:
    key_list = jax.random.split(jax.random.key(seed), 9)
    return {
        "tokens": normal_values(key_list[0], (TOKENS, D), 1.0, 6.0, ((0, 128),)),
        "grad_out": normal_values(key_list[1], (TOKENS, D), 1.0, 6.0, ((0, 128),)),
        "gate_weights": jnp.clip(0.2 + 0.8 * jax.random.uniform(key_list[2], (TOKENS, 2), jnp.float32) ** levels(key_list[2], (TOKENS, 2), ((0, 128),), -0.2, 0.2), 0.2, 1.0),
        "expert_ids": draw_expert_ids(jax.random.fold_in(key_list[8], 71), 0),
        "slot_ids": draw_slot_ids(jax.random.fold_in(key_list[8], 71), 0),
        "counts": draw_counts(jax.random.fold_in(key_list[8], 71), 0),
        "w_in": normal_values(key_list[6], (EXPERTS, D, FF), D ** -0.5, 0.125, ((0, 8), (2, 16))),
        "w_out": normal_values(key_list[7], (EXPERTS, FF, D), FF ** -0.5, 0.0625, ((0, 8), (1, 16))),
    }


def gelu_parts(values):
    cumulative = 0.5 * (1.0 + jax.scipy.special.erf(values * 0.7071067811865476))
    density = values * jnp.exp(-0.5 * values * values) * 0.3989422804014327
    return values * cumulative, cumulative + density


def expert_grads(operands):
    inputs, grads, first_w, second_w = operands
    pre_act = jnp.dot(inputs, first_w, preferred_element_type=jnp.float32)
    activated, slopes = gelu_parts(pre_act)
    hidden = activated.astype(jnp.bfloat16)
    back_hidden = jnp.dot(grads, second_w.T, preferred_element_type=jnp.float32)
    deltas = (back_hidden * slopes).astype(jnp.bfloat16)
    grad_second = jnp.dot(hidden.T, grads, preferred_element_type=jnp.float32)
    grad_first = jnp.dot(inputs.T, deltas, preferred_element_type=jnp.float32)
    grad_inputs = jnp.dot(deltas, first_w.T, preferred_element_type=jnp.float32).astype(jnp.bfloat16)
    return grad_first, grad_second, grad_inputs


def reference(tokens, grad_out, gate_weights, expert_ids, slot_ids, counts, w_in, w_out):
    devices_all = N_NODE * N_LOCAL
    slots_all = devices_all * EXPERTS * CAP
    device_of = (jnp.arange(TOKENS) // TOK_DEV).astype(jnp.int32)
    limits = counts[device_of[:, None], expert_ids]
    is_kept = slot_ids < limits
    flat_index = jnp.where(is_kept, (device_of[:, None] * EXPERTS + expert_ids) * CAP + slot_ids, slots_all).astype(jnp.int32)
    scaled = (gate_weights[:, :, None] * grad_out[:, None, :].astype(jnp.float32)).astype(jnp.bfloat16)
    repeated = jnp.broadcast_to(tokens[:, None, :], (TOKENS, 2, D))
    input_buffer = jnp.zeros((slots_all, D), jnp.bfloat16).at[flat_index.reshape(-1)].set(repeated.reshape(-1, D), mode="drop")
    grad_buffer = jnp.zeros((slots_all, D), jnp.bfloat16).at[flat_index.reshape(-1)].set(scaled.reshape(-1, D), mode="drop")
    input_buffer = jnp.moveaxis(input_buffer.reshape(devices_all, EXPERTS, CAP, D), 1, 0).reshape(EXPERTS, devices_all * CAP, D)
    grad_buffer = jnp.moveaxis(grad_buffer.reshape(devices_all, EXPERTS, CAP, D), 1, 0).reshape(EXPERTS, devices_all * CAP, D)
    grad_first, grad_second, grad_inputs = lax.map(expert_grads, (input_buffer, grad_buffer, w_in, w_out))
    returned = jnp.moveaxis(grad_inputs.reshape(EXPERTS, devices_all, CAP, D), 0, 1).reshape(slots_all, D)
    picked = jnp.take(returned, jnp.minimum(flat_index, slots_all - 1), axis=0).astype(jnp.float32)
    picked = jnp.where(is_kept[:, :, None], picked, jnp.float32(0.0))
    grad_tokens = jnp.sum(picked, axis=1).astype(jnp.bfloat16)
    return grad_tokens, grad_first, grad_second
```

```python
import functools

import jax
import jax.numpy as jnp
from jax import lax
from jax.experimental import pallas as pl
from jax.experimental.pallas import tpu as pltpu
from jax.sharding import PartitionSpec as P

MESH = pl.DeviceIdType.MESH
BF16 = jnp.bfloat16
F32 = jnp.float32

SIDE = 4
CORES = 2
EXPERTS = 8
CAP = 16
NODES = SIDE * SIDE
CHUNKS = SIDE
DX = (0, 1, 3, 2)
RETURN_ORDER = (1, 2, 3, 0)
PART = NODES * CAP
CHUNK = CORES * PART
COLUMN = SIDE * CAP


def gelu_parts(values):
    cumulative = 0.5 * (1.0 + lax.erf(values * 0.7071067811865476))
    density = values * jnp.exp(-0.5 * values * values) * 0.3989422804014327
    return (values * cumulative, cumulative + density)


def turn(value, step):
    return lax.rem(value + step, SIDE)


def kernel(
    tokens, grad_out, gates, ids, slots, counts, w_in, w_out,
    grad_tokens, grad_in, grad_second,
    rows, w1, w2, back, acc_in, acc_out, acc_turned, out_x, out_g, returned, held,
    hidden_t, delta, delta_t, slopes, relay, arrived, relay_block, arrived_block, final,
    load_sem, store_sem, swap_send, swap_recv, gather_send, gather_recv,
    sum_send, sum_recv, home_send, home_recv,
):
    width = rows.shape[1]
    half = width // 2
    units = w2.shape[0]
    node, local = lax.axis_index("node"), lax.axis_index("local")
    y, z = node // SIDE, lax.rem(node, SIDE)
    x, core = local // CORES, lax.rem(local, CORES)

    primary, secondary = (y, z), (z, y)

    def at(part, a, b):
        return a * SIDE + b if part == 0 else b * SIDE + a

    def on_primary(part, step):
        return (at(part, turn(primary[part], step), secondary[part]), local)

    def on_secondary(part, step):
        return (at(part, primary[part], turn(secondary[part], step)), local)

    def block(part, da, db):
        return turn(secondary[part], db) * SIDE + turn(primary[part], da)

    def spot(k, g, part, place):
        return pl.ds(pl.multiple_of(((k * 2 + g) * 2 + part) * PART + place * CAP, CAP), CAP)

    def drain(ref, count, sem):
        view = ref.at[pl.ds(0, count)]
        pltpu.make_async_copy(view, view, sem).wait()

    def push(src, dst, send, recv, device):
        pltpu.make_async_remote_copy(
            src_ref=src, dst_ref=dst, send_sem=send, recv_sem=recv,
            device_id=device, device_id_type=MESH,
        ).start()

    barrier = pltpu.get_barrier_semaphore()
    partners = [on_primary(0, 1), on_primary(0, 3), on_primary(1, 1), on_primary(1, 3)]
    for dx in range(SIDE):
        for flip in range(CORES):
            if dx or flip:
                partners.append((node, turn(x, dx) * CORES + lax.rem(core + flip, CORES)))
    for partner in partners:
        pl.semaphore_signal(barrier, inc=1, device_id=partner, device_id_type=MESH)

    first_load = pltpu.make_async_copy(w_in.at[0], w1, load_sem.at[0])
    second_load = pltpu.make_async_copy(w_out.at[0], w2, load_sem.at[1])
    first_load.start()
    second_load.start()

    limits = counts[...].astype(F32)
    expert_lanes = lax.broadcasted_iota(jnp.int32, (ids.shape[0], EXPERTS), 1)
    slot_lanes = lax.broadcasted_iota(jnp.int32, (ids.shape[0], EXPERTS * CAP), 1)
    picks, weighted = None, None
    for choice in range(2):
        expert = ids[:, choice : choice + 1]
        slot = slots[:, choice : choice + 1]
        limit = jnp.sum(
            jnp.where(expert == expert_lanes, limits, 0.0), axis=1, keepdims=True
        )
        place = jnp.where(slot.astype(F32) < limit, expert * CAP + slot, -1)
        pick = jnp.where(place == slot_lanes, 1.0, 0.0)
        scale = pick * gates[:, choice : choice + 1]
        picks = pick if picks is None else picks + pick
        weighted = scale if weighted is None else weighted + scale
    held[...] = picks.astype(BF16)
    to_slots = picks.T.astype(BF16)
    slot_gate = jnp.sum(weighted.T, axis=1, keepdims=True)
    out_x[...] = jnp.dot(to_slots, tokens[...], preferred_element_type=F32).astype(BF16)
    out_g[...] = (
        slot_gate * jnp.dot(to_slots, grad_out[...], preferred_element_type=F32)
    ).astype(BF16)
    own = pl.ds(pl.multiple_of(local * CAP, CAP), CAP)
    for part in range(CORES):

        @pl.when(core == part)
        def _():
            rows[spot(0, 0, part, block(part, 0, 0)), :] = out_x[own, :]
            rows[spot(0, 1, part, block(part, 0, 0)), :] = out_g[own, :]

    pl.semaphore_wait(barrier, len(partners))

    for k in range(CHUNKS):
        for flip in range(CORES):
            if k or flip:
                target = turn(x, SIDE - DX[k]) * CORES + lax.rem(core + flip, CORES)
                there = pl.ds(pl.multiple_of(target * CAP, CAP), CAP)
                mine = jnp.where(core == 0, block(0, 0, 0), block(1, 0, 0))
                for g, source in enumerate((out_x, out_g)):
                    push(
                        source.at[there], rows.at[spot(k, g, core, mine)],
                        swap_send, swap_recv.at[k, core], (node, target),
                    )

    acc_in[...] = jnp.zeros_like(acc_in)
    acc_out[...] = jnp.zeros_like(acc_out)

    def ship(k, g, part, place, device, event):
        where = rows.at[spot(k, g, part, place)]
        push(where, where, gather_send.at[k], gather_recv.at[k, part, event], device)

    def gather_start(k, first=False):
        for part in range(CORES):
            if first:
                pl.when(core != part)(lambda: drain(rows, 2 * CAP, swap_recv.at[k, part]))
            else:
                drain(rows, 2 * CAP, swap_recv.at[k, part])
            for g in range(2):
                mine = block(part, 0, 0)
                ship(k, g, part, mine, on_primary(part, 1), 0)
                ship(k, g, part, mine, on_primary(part, 3), 1)
            for g in range(2):
                ship(k, g, part, mine, on_secondary(part, 1), 3)
                ship(k, g, part, mine, on_secondary(part, 3), 4)

    def gather_near(k):
        for part in range(CORES):
            drain(rows, 2 * CAP, gather_recv.at[k, part, 0])
            ship(k, 0, part, block(part, 3, 0), on_primary(part, 1), 2)
            drain(rows, 2 * CAP, gather_recv.at[k, part, 1])
            ship(k, 1, part, block(part, 1, 0), on_primary(part, 3), 2)
        for part in range(CORES):
            for da in (3, 1):
                for g in range(2):
                    ship(k, g, part, block(part, da, 0), on_secondary(part, 1), 5)
                    ship(k, g, part, block(part, da, 0), on_secondary(part, 3), 6)

    def gather_far(k):
        for part in range(CORES):
            drain(rows, 2 * CAP, gather_recv.at[k, part, 2])
            for g in range(2):
                ship(k, g, part, block(part, 2, 0), on_secondary(part, 1), 7)
                ship(k, g, part, block(part, 2, 0), on_secondary(part, 3), 8)

    def gather_pass(k, event, steps):
        for part in range(CORES):
            drain(rows, 2 * len(steps) * CAP, gather_recv.at[k, part, event])
            for da in steps:
                ship(k, 0, part, block(part, da, 3), on_secondary(part, 1), 9)
            drain(rows, 2 * len(steps) * CAP, gather_recv.at[k, part, event + 1])
            for da in steps:
                ship(k, 1, part, block(part, da, 1), on_secondary(part, 3), 9)

    def gather_end(k):
        for part in range(CORES):
            drain(rows, 2 * SIDE * CAP, gather_recv.at[k, part, 9])

    def section(k, g, part):
        start = ((k * 2 + g) * 2 + part) * PART
        return pl.ds(pl.multiple_of(start, PART), PART)

    def activate(k, part):
        pre = jnp.dot(rows[section(k, 0, part), :], w1[...], preferred_element_type=F32)
        activated, slope = gelu_parts(pre)
        hidden_t[:, part * PART : (part + 1) * PART] = activated.T.astype(BF16)
        slopes[part * PART : (part + 1) * PART, :] = slope

    def backward(k, part):
        span = slice(part * PART, (part + 1) * PART)
        back_hidden = lax.dot_general(
            rows[section(k, 1, part), :], w2[...], (((1,), (1,)), ((), ())),
            preferred_element_type=F32,
        )
        change = back_hidden * slopes[span, :]
        delta[span, :] = change.astype(BF16)
        delta_t[:, span] = change.T.astype(BF16)

    def to_inputs(k, part):
        span = slice(part * PART, (part + 1) * PART)
        for start in range(0, width, units):
            back[
                pl.ds(pl.multiple_of(k * CHUNK + part * PART, PART), PART), start : start + units
            ] = lax.dot_general(
                delta[span, :], w1[start : start + units, :], (((1,), (1,)), ((), ())),
                preferred_element_type=F32,
            ).astype(BF16)

    def to_weights(k, g, left, total, start):
        span = pl.ds(pl.multiple_of((k * 2 + g) * CHUNK, CHUNK), CHUNK)
        total[:, start : start + units] += jnp.dot(
            left[...], rows[span, start : start + units], preferred_element_type=F32
        )

    def pieces(k):
        done = []
        for part in range(CORES):
            done.append(functools.partial(activate, k, part))
        for part in range(CORES):
            done.append(functools.partial(backward, k, part))
        for part in range(CORES):
            done.append(functools.partial(to_inputs, k, part))
        for g, left, total in ((1, hidden_t, acc_out), (0, delta_t, acc_in)):
            for start in range(0, width, units):
                done.append(functools.partial(to_weights, k, g, left, total, start))
        return done

    def run(work, count):
        for _ in range(min(count, len(work))):
            work.pop(0)()

    gather_start(0, first=True)
    first_load.wait()
    second_load.wait()

    @pl.loop(0, CHUNKS)
    def _(k):
        def compute(count):
            @pl.when(k > 0)
            def _():
                run(work, count)

        work = pieces(k - 1)
        gather_near(k)
        compute(3)
        gather_pass(k, 3, (0,))
        compute(2)
        gather_far(k)

        @pl.when(k < CHUNKS - 1)
        def _():
            gather_start(k + 1)

        compute(3)
        gather_pass(k, 5, (3, 1))
        compute(3)
        gather_pass(k, 7, (2,))
        compute(3)
        gather_end(k)

    def strip(k, part, db, low, high):
        start = k * CHUNK + part * PART + turn(secondary[part], db) * COLUMN + low
        return pl.ds(pl.multiple_of(start, CAP), high - low)

    middle = COLUMN // 2

    def column_start(k):
        for part in range(CORES):
            for side, step in ((0, 1), (1, 3)):
                low, high = ((0, middle), (middle, COLUMN))[side]
                push(
                    back.at[strip(k, part, 2, low, high)], relay.at[k, part, side],
                    sum_send.at[k], sum_recv.at[k, part, side], on_secondary(part, step),
                )
            for side, step in ((0, 1), (1, 3)):
                low, high = ((middle, COLUMN), (0, middle))[side]
                push(
                    back.at[strip(k, part, step, low, high)],
                    arrived.at[k, part, side, pl.ds(low, middle)],
                    sum_send.at[k], sum_recv.at[k, part, 2 + side], on_secondary(part, step),
                )

    def column_pass(k):
        for part in range(CORES):
            for side, step in ((0, 1), (1, 3)):
                low, high = ((0, middle), (middle, COLUMN))[side]
                where = strip(k, part, step, low, high)
                drain(back, middle, sum_recv.at[k, part, side])
                back[where, :] = (
                    back[where, :].astype(F32) + relay[k, part, side].astype(F32)
                ).astype(BF16)
                push(
                    back.at[where], arrived.at[k, part, side, pl.ds(low, middle)],
                    sum_send.at[k], sum_recv.at[k, part, 2 + side], on_secondary(part, step),
                )

    def lump(k, part, da):
        start = k * CHUNK + part * PART + block(part, da, 0) * CAP
        return pl.ds(pl.multiple_of(start, CAP), CAP)

    lanes = (pl.ds(0, half), pl.ds(half, half))

    def column_end(k):
        for part in range(CORES):
            drain(back, COLUMN, sum_recv.at[k, part, 2])
            drain(back, COLUMN, sum_recv.at[k, part, 3])
            where = strip(k, part, 0, 0, COLUMN)
            back[where, :] = (
                back[where, :].astype(F32)
                + arrived[k, part, 0].astype(F32)
                + arrived[k, part, 1].astype(F32)
            ).astype(BF16)
            for side, step in ((0, 1), (1, 3)):
                push(
                    back.at[lump(k, part, 2), lanes[side]], relay_block.at[k, part, side],
                    sum_send.at[k], sum_recv.at[k, part, 4 + side], on_primary(part, step),
                )
            for side, step in ((0, 1), (1, 3)):
                push(
                    back.at[lump(k, part, step), lanes[1 - side]],
                    arrived_block.at[k, part, side, :, lanes[1 - side]],
                    sum_send.at[k], sum_recv.at[k, part, 6 + side], on_primary(part, step),
                )

    def block_pass(k):
        for part in range(CORES):
            for side, step in ((0, 1), (1, 3)):
                where = lump(k, part, step)
                pltpu.make_async_copy(
                    relay_block.at[k, part, side], relay_block.at[k, part, side],
                    sum_recv.at[k, part, 4 + side],
                ).wait()
                back[where, lanes[side]] = (
                    back[where, lanes[side]].astype(F32) + relay_block[k, part, side].astype(F32)
                ).astype(BF16)
                push(
                    back.at[where, lanes[side]], arrived_block.at[k, part, side, :, lanes[side]],
                    sum_send.at[k], sum_recv.at[k, part, 6 + side], on_primary(part, step),
                )

    def block_end(k):
        for part in range(CORES):
            drain(back, CAP, sum_recv.at[k, part, 6])
            drain(back, CAP, sum_recv.at[k, part, 7])
            total = (
                back[lump(k, part, 0), :].astype(F32)
                + arrived_block[k, part, 0].astype(F32)
                + arrived_block[k, part, 1].astype(F32)
            ).astype(BF16)
            target = (node, turn(x, DX[k]) * CORES + part)

            def keep():
                returned[own, :] = total

            def send():
                final[k, part] = total
                push(
                    final.at[k, part], returned.at[own],
                    home_send, home_recv.at[k, core], target,
                )

            if k == 0:
                pl.when(core == part)(keep)
                pl.when(core != part)(send)
            else:
                send()

    work = pieces(CHUNKS - 1)
    r0, r1, r2, r3 = RETURN_ORDER
    column_start(r0)
    column_start(r1)
    run(work, 2)
    column_pass(r0)
    run(work, 2)
    column_pass(r1)
    run(work, 2)
    column_end(r0)
    column_start(r2)
    run(work, 2)
    column_end(r1)
    block_pass(r0)
    run(work, 2)
    column_pass(r2)
    column_start(r3)
    run(work, 2)
    block_end(r0)
    block_pass(r1)
    run(work, 2)
    first_store = pltpu.make_async_copy(acc_out, grad_second.at[0], store_sem.at[0])
    first_store.start()
    column_end(r2)
    column_pass(r3)
    block_end(r1)
    block_pass(r2)
    for start in range(0, width, units):
        acc_turned[start : start + units, :] = acc_in[:, start : start + units].T
    second_store = pltpu.make_async_copy(acc_turned, grad_in.at[0], store_sem.at[1])
    second_store.start()
    column_end(r3)
    block_end(r2)
    block_pass(r3)
    block_end(r3)

    for k in range(CHUNKS):
        for part in range(CORES):
            if k:
                drain(back, CAP, home_recv.at[k, part])
            else:
                pl.when(core != part)(lambda: drain(back, CAP, home_recv.at[k, part]))
    grad_tokens[...] = jnp.dot(
        held[...], returned[...], preferred_element_type=F32
    ).astype(BF16)

    first_store.wait()
    second_store.wait()
    drain(rows, 2 * (EXPERTS - 1) * CAP, swap_send)
    drain(rows, (EXPERTS - 1) * CAP, home_send)
    for k in range(CHUNKS):
        drain(rows, CORES * 30 * CAP, gather_send.at[k])
        drain(rows, CORES * 15 * CAP, sum_send.at[k])


def body(tokens, grad_out, gate_weights, expert_ids, slot_ids, counts, w_in, w_out):
    token_rows, width = tokens.shape
    units = w_out.shape[1]
    in_vmem = pl.BlockSpec(memory_space=pltpu.VMEM)
    in_hbm = pl.BlockSpec(memory_space=pl.ANY)
    dma = pltpu.SemaphoreType.DMA
    return pl.pallas_call(
        kernel,
        out_shape=(
            jax.ShapeDtypeStruct(tokens.shape, BF16),
            jax.ShapeDtypeStruct(w_in.shape, F32),
            jax.ShapeDtypeStruct(w_out.shape, F32),
        ),
        in_specs=[in_vmem] * 6 + [in_hbm] * 2,
        out_specs=(in_vmem, in_hbm, in_hbm),
        scratch_shapes=[
            pltpu.VMEM((CHUNKS * 2 * CHUNK, width), BF16),
            pltpu.VMEM((width, units), BF16),
            pltpu.VMEM((units, width), BF16),
            pltpu.VMEM((CHUNKS * CHUNK, width), BF16),
            pltpu.VMEM((units, width), F32),
            pltpu.VMEM((units, width), F32),
            pltpu.VMEM((width, units), F32),
            pltpu.VMEM((EXPERTS * CAP, width), BF16),
            pltpu.VMEM((EXPERTS * CAP, width), BF16),
            pltpu.VMEM((EXPERTS * CAP, width), BF16),
            pltpu.VMEM((token_rows, EXPERTS * CAP), BF16),
            pltpu.VMEM((units, CHUNK), BF16),
            pltpu.VMEM((CHUNK, units), BF16),
            pltpu.VMEM((units, CHUNK), BF16),
            pltpu.VMEM((CHUNK, units), F32),
            pltpu.VMEM((CHUNKS, CORES, 2, COLUMN // 2, width), BF16),
            pltpu.VMEM((CHUNKS, CORES, 2, COLUMN, width), BF16),
            pltpu.VMEM((CHUNKS, CORES, 2, CAP, width // 2), BF16),
            pltpu.VMEM((CHUNKS, CORES, 2, CAP, width), BF16),
            pltpu.VMEM((CHUNKS, CORES, CAP, width), BF16),
            dma((2,)),
            dma((2,)),
            dma,
            dma((CHUNKS, CORES)),
            dma((CHUNKS,)),
            dma((CHUNKS, CORES, 10)),
            dma((CHUNKS,)),
            dma((CHUNKS, CORES, 8)),
            dma,
            dma((CHUNKS, CORES)),
        ],
        compiler_params=pltpu.CompilerParams(
            collective_id=0, has_side_effects=True, vmem_limit_bytes=62 * 2**20
        ),
        cost_estimate=pl.CostEstimate(
            flops=10 * NODES * EXPERTS * CAP * width * units,
            bytes_accessed=16 * width * units,
            transcendentals=0,
        ),
    )(tokens, grad_out, gate_weights, expert_ids, slot_ids, counts, w_in, w_out)


def solution(mesh):
    placed = (
        P(("node", "local"), None),
        P(("node", "local"), None),
        P(("node", "local"), None),
        P(("node", "local"), None),
        P(("node", "local"), None),
        P(("node", "local"), None),
        P("local", None, "node"),
        P("local", "node", None),
    )
    return jax.shard_map(
        body,
        mesh=mesh,
        in_specs=placed,
        out_specs=(P(("node", "local"), None), P("local", None, "node"), P("local", "node", None)),
        check_vma=False,
    )
```

```python
import functools

import jax
import jax.numpy as jnp
from jax import lax
from jax.experimental import pallas as pl
from jax.experimental.pallas import tpu as pltpu
from jax.sharding import PartitionSpec as P

MESH = pl.DeviceIdType.MESH
BF16 = jnp.bfloat16
F32 = jnp.float32

SIDE = 4
CORES = 2
EXPERTS = 8
CAP = 16
NODES = SIDE * SIDE
CHUNKS = SIDE
DX = (0, 1, 2, 3)
RETURN_ORDER = (1, 2, 0, 3)
PIECES = 4
PART = NODES * CAP
CHUNK = CORES * PART
COLUMN = SIDE * CAP


def gelu_parts(values):
    cumulative = 0.5 * (1.0 + lax.erf(values * 0.7071067811865476))
    density = values * jnp.exp(-0.5 * values * values) * 0.3989422804014327
    return (values * cumulative, cumulative + density)


def turn(value, step):
    return lax.rem(value + step, SIDE)


def kernel(
    tokens, grad_out, gates, ids, slots, counts, w_in, w_out,
    picked_out, returned_out, grad_in, grad_second,
    rows, w1, w2, back, turned, rounded, out_x, out_g, returned, held,
    hidden_t, delta, delta_t, slopes, relay, arrived, relay_block, arrived_block, across, final,
    load_sem, store_sem, swap_send, swap_recv, gather_send, gather_recv,
    sum_send, sum_recv, home_send, home_recv,
):
    width = rows.shape[1]
    half = width // 2
    units = w2.shape[0]
    node, local = lax.axis_index("node"), lax.axis_index("local")
    y, z = node // SIDE, lax.rem(node, SIDE)
    x, core = local // CORES, lax.rem(local, CORES)

    primary, secondary = (y, z), (z, y)

    def at(part, a, b):
        return a * SIDE + b if part == 0 else b * SIDE + a

    def on_primary(part, step):
        return (at(part, turn(primary[part], step), secondary[part]), local)

    def on_secondary(part, step):
        return (at(part, primary[part], turn(secondary[part], step)), local)

    def block(part, da, db):
        return turn(secondary[part], db) * SIDE + turn(primary[part], da)

    def spot(k, g, part, place):
        return pl.ds(pl.multiple_of(((k * 2 + g) * 2 + part) * PART + place * CAP, CAP), CAP)

    def drain(ref, count, sem):
        view = ref.at[pl.ds(0, count)]
        pltpu.make_async_copy(view, view, sem).wait()

    def push(src, dst, send, recv, device):
        pltpu.make_async_remote_copy(
            src_ref=src, dst_ref=dst, send_sem=send, recv_sem=recv,
            device_id=device, device_id_type=MESH,
        ).start()

    barrier = pltpu.get_barrier_semaphore()
    partners = [on_primary(part, step) for part in range(CORES) for step in (1, 2, 3)]
    for dx in range(SIDE):
        for flip in range(CORES):
            if dx or flip:
                partners.append((node, turn(x, dx) * CORES + lax.rem(core + flip, CORES)))
    for partner in partners:
        pl.semaphore_signal(barrier, inc=1, device_id=partner, device_id_type=MESH)

    first_load = pltpu.make_async_copy(w_in.at[0], w1, load_sem.at[0])
    second_load = pltpu.make_async_copy(w_out.at[0], w2, load_sem.at[1])
    first_load.start()
    second_load.start()

    limits = counts[...].astype(F32)
    expert_lanes = lax.broadcasted_iota(jnp.int32, (ids.shape[1], EXPERTS), 1)
    slot_lanes = lax.broadcasted_iota(jnp.int32, (ids.shape[1], EXPERTS * CAP), 1)
    picks, weighted = None, None
    ids_down, slots_down, gates_down = (
        jnp.concatenate([ref[...].astype(F32)] * 4, axis=0).T for ref in (ids, slots, gates)
    )
    for choice in range(2):
        expert = ids_down[:, choice : choice + 1].astype(jnp.int32)
        slot = slots_down[:, choice : choice + 1].astype(jnp.int32)
        limit = jnp.sum(
            jnp.where(expert == expert_lanes, limits, 0.0), axis=1, keepdims=True
        )
        place = jnp.where(slot.astype(F32) < limit, expert * CAP + slot, -1)
        pick = jnp.where(place == slot_lanes, 1.0, 0.0)
        scale = pick * gates_down[:, choice : choice + 1]
        picks = pick if picks is None else picks + pick
        weighted = scale if weighted is None else weighted + scale
    held[...] = picks.astype(BF16)
    to_slots = picks.T.astype(BF16)
    slot_gate = jnp.sum(weighted.T, axis=1, keepdims=True)
    out_x[...] = jnp.dot(to_slots, tokens[...], preferred_element_type=F32).astype(BF16)
    out_g[...] = (
        slot_gate * jnp.dot(to_slots, grad_out[...], preferred_element_type=F32)
    ).astype(BF16)
    own = pl.ds(pl.multiple_of(local * CAP, CAP), CAP)
    for part in range(CORES):

        @pl.when(core == part)
        def _():
            rows[spot(0, 0, part, block(part, 0, 0)), :] = out_x[own, :]
            rows[spot(0, 1, part, block(part, 0, 0)), :] = out_g[own, :]

    pl.semaphore_wait(barrier, len(partners))

    def swap(k, flip):
        target = turn(x, SIDE - DX[k]) * CORES + lax.rem(core + flip, CORES)
        there = pl.ds(pl.multiple_of(target * CAP, CAP), CAP)
        mine = jnp.where(core == 0, block(0, 0, 0), block(1, 0, 0))
        for g, source in enumerate((out_x, out_g)):
            push(
                source.at[there], rows.at[spot(k, g, core, mine)],
                swap_send, swap_recv.at[k, core], (node, target),
            )

    def ship(k, g, part, place, device, event):
        where = rows.at[spot(k, g, part, place)]
        push(where, where, gather_send.at[k], gather_recv.at[k, part, event], device)

    def gather_own(k, part):
        mine = block(part, 0, 0)
        for g in range(2):
            ship(k, g, part, mine, on_primary(part, 1), 0)
            ship(k, g, part, mine, on_primary(part, 3), 1)
        for g in range(2):
            ship(k, g, part, mine, on_secondary(part, 1), 3)
            ship(k, g, part, mine, on_secondary(part, 3), 4)

    def gather_start(k):
        for part in range(CORES):
            drain(rows, 2 * CAP, swap_recv.at[k, part])
            gather_own(k, part)

    def gather_near(k):
        for part in range(CORES):
            drain(rows, 2 * CAP, gather_recv.at[k, part, 0])
            ship(k, 0, part, block(part, 3, 0), on_primary(part, 1), 2)
            drain(rows, 2 * CAP, gather_recv.at[k, part, 1])
            ship(k, 1, part, block(part, 1, 0), on_primary(part, 3), 2)
        for part in range(CORES):
            for da in (3, 1):
                for g in range(2):
                    ship(k, g, part, block(part, da, 0), on_secondary(part, 1), 5)
                    ship(k, g, part, block(part, da, 0), on_secondary(part, 3), 6)

    def gather_far(k):
        for part in range(CORES):
            drain(rows, 2 * CAP, gather_recv.at[k, part, 2])
            for g in range(2):
                ship(k, g, part, block(part, 2, 0), on_secondary(part, 1), 7)
                ship(k, g, part, block(part, 2, 0), on_secondary(part, 3), 8)

    def gather_pass(k, event, steps):
        for part in range(CORES):
            drain(rows, 2 * len(steps) * CAP, gather_recv.at[k, part, event])
            for da in steps:
                ship(k, 0, part, block(part, da, 3), on_secondary(part, 1), 9)
            drain(rows, 2 * len(steps) * CAP, gather_recv.at[k, part, event + 1])
            for da in steps:
                ship(k, 1, part, block(part, da, 1), on_secondary(part, 3), 9)

    def gather_end(k):
        for part in range(CORES):
            drain(rows, 2 * SIDE * CAP, gather_recv.at[k, part, 9])

    def section(k, g, part):
        start = ((k * 2 + g) * 2 + part) * PART
        return pl.ds(pl.multiple_of(start, PART), PART)

    def span_of(k, part):
        return pl.ds(pl.multiple_of(k * CHUNK + part * PART, PART), PART)

    def activate(k, part):
        pre = jnp.dot(rows[section(k, 0, part), :], w1[...], preferred_element_type=F32)
        activated, slope = gelu_parts(pre)
        hidden_t[:, span_of(k, part)] = activated.T.astype(BF16)
        slopes[part * PART : (part + 1) * PART, :] = slope

    def backward(k, part):
        span = slice(part * PART, (part + 1) * PART)
        back_hidden = lax.dot_general(
            rows[section(k, 1, part), :], w2[...], (((1,), (1,)), ((), ())),
            preferred_element_type=F32,
        )
        change = back_hidden * slopes[span, :]
        delta[span, :] = change.astype(BF16)
        delta_t[:, span_of(k, part)] = change.T.astype(BF16)

    def to_inputs(k, part):
        span = slice(part * PART, (part + 1) * PART)
        for start in range(0, width, units):
            back[span_of(k, part), start : start + units] = lax.dot_general(
                delta[span, :], w1[start : start + units, :], (((1,), (1,)), ((), ())),
                preferred_element_type=F32,
            ).astype(BF16)

    def pieces(k):
        return [
            functools.partial(piece, k, part)
            for piece in (activate, backward, to_inputs)
            for part in range(CORES)
        ]

    def product(left, g, start):
        total = None
        for k in range(CHUNKS):
            term = jnp.dot(
                left[:, k * CHUNK : (k + 1) * CHUNK],
                rows[pl.ds((k * 2 + g) * CHUNK, CHUNK), start : start + units],
                preferred_element_type=F32,
            )
            total = term if total is None else total + term
        return total

    def second_weights(start):
        rounded[:, start : start + units] = product(hidden_t, 1, start).astype(BF16)

    def first_weights(start):
        turned[start : start + units, :] = product(delta_t, 0, start).T.astype(BF16)

    def run(work, count):
        for _ in range(min(count, len(work))):
            work.pop(0)()

    swap(0, 1)
    for part in range(CORES):
        pl.when(core == part)(functools.partial(gather_own, 0, part))
    for k in range(1, CHUNKS):
        for flip in range(CORES):
            swap(k, flip)
    for part in range(CORES):

        @pl.when(core != part)
        def _():
            drain(rows, 2 * CAP, swap_recv.at[0, part])
            gather_own(0, part)

    first_load.wait()
    second_load.wait()

    @pl.loop(0, CHUNKS)
    def _(k):
        work = pieces(k - 1)

        def after_first(step):
            pl.when(k > 0)(step)

        gather_near(k)
        after_first(lambda: gather_pass(k - 1, 7, (2,)))
        pl.when(k < CHUNKS - 1)(lambda: gather_start(k + 1))
        gather_pass(k, 3, (0,))
        after_first(lambda: gather_end(k - 1))
        after_first(lambda: run(work, 2))
        gather_far(k)
        after_first(lambda: run(work, 2))
        gather_pass(k, 5, (3, 1))
        after_first(lambda: run(work, 2))

    gather_pass(CHUNKS - 1, 7, (2,))

    def strip(k, part, db, low, high):
        start = k * CHUNK + part * PART + turn(secondary[part], db) * COLUMN + low
        return pl.ds(pl.multiple_of(start, CAP), high - low)

    middle = COLUMN // 2

    def column_start(k):
        for part in range(CORES):
            for side, step in ((0, 1), (1, 3)):
                low, high = ((0, middle), (middle, COLUMN))[side]
                push(
                    back.at[strip(k, part, 2, low, high)], relay.at[k, part, side],
                    sum_send.at[k], sum_recv.at[k, part, side], on_secondary(part, step),
                )
            for side, step in ((0, 1), (1, 3)):
                low, high = ((middle, COLUMN), (0, middle))[side]
                push(
                    back.at[strip(k, part, step, low, high)],
                    arrived.at[k, part, side, pl.ds(low, middle)],
                    sum_send.at[k], sum_recv.at[k, part, 2 + side], on_secondary(part, step),
                )

    def column_pass(k):
        for part in range(CORES):
            for side, step in ((0, 1), (1, 3)):
                low, high = ((0, middle), (middle, COLUMN))[side]
                where = strip(k, part, step, low, high)
                drain(back, middle, sum_recv.at[k, part, side])
                back[where, :] = (
                    back[where, :].astype(F32) + relay[k, part, side].astype(F32)
                ).astype(BF16)
                push(
                    back.at[where], arrived.at[k, part, side, pl.ds(low, middle)],
                    sum_send.at[k], sum_recv.at[k, part, 2 + side], on_secondary(part, step),
                )

    def lump(k, part, da):
        start = k * CHUNK + part * PART + block(part, da, 0) * CAP
        return pl.ds(pl.multiple_of(start, CAP), CAP)

    lanes = (pl.ds(0, half), pl.ds(half, half))

    def column_add(k, part):
        drain(back, COLUMN, sum_recv.at[k, part, 2])
        drain(back, COLUMN, sum_recv.at[k, part, 3])
        where = strip(k, part, 0, 0, COLUMN)
        back[where, :] = (
            back[where, :].astype(F32)
            + arrived[k, part, 0].astype(F32)
            + arrived[k, part, 1].astype(F32)
        ).astype(BF16)

    def column_end(k):
        for part in range(CORES):
            column_add(k, part)
            for side, step in ((0, 1), (1, 3)):
                push(
                    back.at[lump(k, part, 2), lanes[side]], relay_block.at[k, part, side],
                    sum_send.at[k], sum_recv.at[k, part, 4 + side], on_primary(part, step),
                )
            for side, step in ((0, 1), (1, 3)):
                push(
                    back.at[lump(k, part, step), lanes[1 - side]],
                    arrived_block.at[k, part, side, :, lanes[1 - side]],
                    sum_send.at[k], sum_recv.at[k, part, 6 + side], on_primary(part, step),
                )

    def column_last(k):
        for part in range(CORES):
            column_add(k, part)
            push(
                back.at[lump(k, part, 2)], across.at[part],
                sum_send.at[k], sum_recv.at[k, part, 4], on_primary(part, 2),
            )
            for side, step in ((0, 1), (1, 3)):
                push(
                    back.at[lump(k, part, step)], arrived_block.at[k, part, side],
                    sum_send.at[k], sum_recv.at[k, part, 6 + side], on_primary(part, step),
                )

    def block_pass(k):
        for part in range(CORES):
            for side, step in ((0, 1), (1, 3)):
                where = lump(k, part, step)
                pltpu.make_async_copy(
                    relay_block.at[k, part, side], relay_block.at[k, part, side],
                    sum_recv.at[k, part, 4 + side],
                ).wait()
                back[where, lanes[side]] = (
                    back[where, lanes[side]].astype(F32) + relay_block[k, part, side].astype(F32)
                ).astype(BF16)
                push(
                    back.at[where, lanes[side]], arrived_block.at[k, part, side, :, lanes[side]],
                    sum_send.at[k], sum_recv.at[k, part, 6 + side], on_primary(part, step),
                )

    def block_end(k, direct=False):
        for part in range(CORES):
            drain(back, CAP, sum_recv.at[k, part, 6])
            drain(back, CAP, sum_recv.at[k, part, 7])
            total = (
                back[lump(k, part, 0), :].astype(F32)
                + arrived_block[k, part, 0].astype(F32)
                + arrived_block[k, part, 1].astype(F32)
            )
            if direct:
                drain(back, CAP, sum_recv.at[k, part, 4])
                total = total + across[part].astype(F32)
            total = total.astype(BF16)
            target = (node, turn(x, DX[k]) * CORES + part)

            def keep():
                returned[own, :] = total

            def send():
                final[k, part] = total
                push(
                    final.at[k, part], returned.at[own],
                    home_send, home_recv.at[k, core], target,
                )

            if k == 0:
                pl.when(core == part)(keep)
                pl.when(core != part)(send)
            else:
                send()

    work = pieces(CHUNKS - 1)
    column_start(1)
    column_start(2)
    column_start(0)
    gather_end(CHUNKS - 1)
    run(work, 2)
    column_pass(1)
    run(work, 2)
    column_pass(2)
    run(work, 2)
    column_start(3)
    column_end(1)
    column_pass(0)
    second_weights(0 * units)
    block_pass(1)
    column_end(2)
    second_weights(1 * units)
    column_pass(3)
    block_end(1)
    block_pass(2)
    column_end(0)
    second_weights(2 * units)
    block_end(2)
    block_pass(0)
    second_weights(3 * units)
    column_last(3)
    first_weights(0 * units)
    first_weights(1 * units)
    block_end(0)
    first_weights(2 * units)
    first_weights(3 * units)
    stores = [
        pltpu.make_async_copy(ref, out, store_sem.at[i])
        for i, (ref, out) in enumerate(
            ((rounded, grad_second), (turned, grad_in), (held, picked_out))
        )
    ]
    for store in stores:
        store.start()
    block_end(3, direct=True)

    for k in range(CHUNKS):
        for part in range(CORES):
            if k:
                drain(back, CAP, home_recv.at[k, part])
            else:
                pl.when(core != part)(lambda: drain(back, CAP, home_recv.at[k, part]))
    last = pltpu.make_async_copy(returned, returned_out, store_sem.at[3])
    last.start()
    drain(rows, 2 * (EXPERTS - 1) * CAP, swap_send)
    drain(rows, (EXPERTS - 1) * CAP, home_send)
    for k in range(CHUNKS):
        drain(rows, CORES * 30 * CAP, gather_send.at[k])
        drain(rows, CORES * (15 if k != RETURN_ORDER[-1] else 15) * CAP, sum_send.at[k])
    for store in stores:
        store.wait()
    last.wait()


def finish(
    picked, returned, turned, rounded,
    grad_tokens, grad_in, grad_second,
    from_first, from_second, to_first, to_second, rows, held, total, load_sem, store_sem,
):
    loads, stores = [], []
    for source, near in ((picked, held), (returned, rows)):
        loads.append(pltpu.make_async_copy(source, near, load_sem.at[len(loads)]))
    for source, near in ((turned, from_first), (rounded, from_second)):
        height = source.shape[0] // PIECES
        for piece in range(PIECES):
            span = pl.ds(piece * height, height)
            loads.append(
                pltpu.make_async_copy(source.at[span], near.at[span], load_sem.at[len(loads)])
            )
    for load in loads:
        load.start()

    def store(near, target):
        stores.append(pltpu.make_async_copy(near, target, store_sem.at[len(stores)]))
        stores[-1].start()

    for load in loads[:2]:
        load.wait()
    total[...] = jnp.dot(held[...], rows[...], preferred_element_type=F32).astype(BF16)
    store(total, grad_tokens)
    arrivals = iter(loads[2:])
    for near, wide, target in (
        (from_first, to_first, grad_in), (from_second, to_second, grad_second),
    ):
        height = near.shape[0] // PIECES
        for piece in range(PIECES):
            span = pl.ds(piece * height, height)
            next(arrivals).wait()
            wide[span, :] = near[span, :].astype(F32)
            store(wide.at[span], target.at[0, span])
    for started in stores:
        started.wait()


def body(tokens, grad_out, gate_weights, expert_ids, slot_ids, counts, w_in, w_out):
    token_rows, width = tokens.shape
    units = w_out.shape[1]
    in_vmem = pl.BlockSpec(memory_space=pltpu.VMEM)
    in_hbm = pl.BlockSpec(memory_space=pl.ANY)
    dma = pltpu.SemaphoreType.DMA
    slots = EXPERTS * CAP
    results = pl.pallas_call(
        kernel,
        out_shape=(
            jax.ShapeDtypeStruct((token_rows, slots), BF16),
            jax.ShapeDtypeStruct((slots, width), BF16),
            jax.ShapeDtypeStruct((width, units), BF16),
            jax.ShapeDtypeStruct((units, width), BF16),
        ),
        in_specs=[in_vmem] * 6 + [in_hbm] * 2,
        out_specs=(in_hbm,) * 4,
        scratch_shapes=[
            pltpu.VMEM((CHUNKS * 2 * CHUNK, width), BF16),
            pltpu.VMEM((width, units), BF16),
            pltpu.VMEM((units, width), BF16),
            pltpu.VMEM((CHUNKS * CHUNK, width), BF16),
            pltpu.VMEM((width, units), BF16),
            pltpu.VMEM((units, width), BF16),
            pltpu.VMEM((EXPERTS * CAP, width), BF16),
            pltpu.VMEM((EXPERTS * CAP, width), BF16),
            pltpu.VMEM((EXPERTS * CAP, width), BF16),
            pltpu.VMEM((token_rows, EXPERTS * CAP), BF16),
            pltpu.VMEM((units, CHUNKS * CHUNK), BF16),
            pltpu.VMEM((CHUNK, units), BF16),
            pltpu.VMEM((units, CHUNKS * CHUNK), BF16),
            pltpu.VMEM((CHUNK, units), F32),
            pltpu.VMEM((CHUNKS, CORES, 2, COLUMN // 2, width), BF16),
            pltpu.VMEM((CHUNKS, CORES, 2, COLUMN, width), BF16),
            pltpu.VMEM((CHUNKS, CORES, 2, CAP, width // 2), BF16),
            pltpu.VMEM((CHUNKS, CORES, 2, CAP, width), BF16),
            pltpu.VMEM((CORES, CAP, width), BF16),
            pltpu.VMEM((CHUNKS, CORES, CAP, width), BF16),
            dma((2,)),
            dma((4,)),
            dma,
            dma((CHUNKS, CORES)),
            dma((CHUNKS,)),
            dma((CHUNKS, CORES, 10)),
            dma((CHUNKS,)),
            dma((CHUNKS, CORES, 8)),
            dma,
            dma((CHUNKS, CORES)),
        ],
        compiler_params=pltpu.CompilerParams(
            collective_id=0, has_side_effects=True, vmem_limit_bytes=62 * 2**20
        ),
        cost_estimate=pl.CostEstimate(
            flops=10 * NODES * EXPERTS * CAP * width * units,
            bytes_accessed=16 * width * units,
            transcendentals=0,
        ),
    )(tokens, grad_out, gate_weights.T, expert_ids.T, slot_ids.T, counts, w_in, w_out)
    return pl.pallas_call(
        finish,
        out_shape=(
            jax.ShapeDtypeStruct(tokens.shape, BF16),
            jax.ShapeDtypeStruct(w_in.shape, F32),
            jax.ShapeDtypeStruct(w_out.shape, F32),
        ),
        in_specs=[in_hbm] * 4,
        out_specs=(in_hbm,) * 3,
        scratch_shapes=[
            pltpu.VMEM((width, units), BF16),
            pltpu.VMEM((units, width), BF16),
            pltpu.VMEM((width, units), F32),
            pltpu.VMEM((units, width), F32),
            pltpu.VMEM((slots, width), BF16),
            pltpu.VMEM((token_rows, slots), BF16),
            pltpu.VMEM((token_rows, width), BF16),
            dma((2 + 2 * PIECES,)),
            dma((1 + 2 * PIECES,)),
        ],
        compiler_params=pltpu.CompilerParams(vmem_limit_bytes=62 * 2**20),
    )(*results)


def solution(mesh):
    placed = (
        P(("node", "local"), None),
        P(("node", "local"), None),
        P(("node", "local"), None),
        P(("node", "local"), None),
        P(("node", "local"), None),
        P(("node", "local"), None),
        P("local", None, "node"),
        P("local", "node", None),
    )
    return jax.shard_map(
        body,
        mesh=mesh,
        in_specs=placed,
        out_specs=(P(("node", "local"), None), P("local", None, "node"), P("local", "node", None)),
        check_vma=False,
    )
```

```python
import functools

import jax
import jax.numpy as jnp
from jax import lax
from jax.experimental import pallas as pl
from jax.experimental.pallas import tpu as pltpu
from jax.sharding import PartitionSpec as P

MESH = pl.DeviceIdType.MESH
BF16 = jnp.bfloat16
F32 = jnp.float32

SIDE = 4
CORES = 2
EXPERTS = 8
CAP = 16
NODES = SIDE * SIDE
CHUNKS = SIDE
DX = (0, 1, 3, 2)
PAIR = 2 * CAP
PART = NODES * CAP
CHUNK = CORES * PART
PIECES = 4
TILES = 4


def gelu_parts(values):
    cumulative = 0.5 * (1.0 + lax.erf(values * 0.7071067811865476))
    density = values * jnp.exp(-0.5 * values * values) * 0.3989422804014327
    return (values * cumulative, cumulative + density)


def turn(value, step):
    return lax.rem(value + step, SIDE)


def kernel(
    tokens, grad_out, gates, ids, slots, counts, w_in, w_out,
    picked_out, returned_out, grad_in, grad_second,
    rows, w1, w2, back, other_core, turned, rounded, out_x, out_g, returned, held,
    hidden_t, delta, delta_t, slopes, sum_a, sum_b, sum_c, sum_d, sum_e, final,
    weight_send, weight_recv, store_sem, swap_send, swap_recv,
    gather_send, gather_recv, core_send, core_recv,
    add_send, add_recv, sum_send, sum_recv, grad_send, grad_recv, home_send, home_recv,
):
    width = rows.shape[1]
    units = w2.shape[0]
    tile = width // TILES
    node, local = lax.axis_index("node"), lax.axis_index("local")
    y, z = node // SIDE, lax.rem(node, SIDE)
    x, core = local // CORES, lax.rem(local, CORES)

    side = lax.rem((y + 1) // 2, 2)
    half_y = y // 2
    mate_y = y + 1 - 2 * lax.rem(y, 2)
    guest = core != side

    def turn(value, step):
        return lax.rem(value + step, SIDE)

    sibling = (node, x * CORES + 1 - core)
    across = ((SIDE - 1 - y) * SIDE + z, local)
    above = (y * SIDE + turn(z, 1), local)
    below = (y * SIDE + turn(z, 3), local)
    trade = (mate_y * SIDE + z, x * CORES + 1 - core)

    def peer(mate, step):
        there = mate_y if mate else y
        return (there * SIDE + z, turn(x, step) * CORES + core)

    def spot(k, g, low_y, at_z, count):
        start = ((k * 2 + g) * 2 + core) * PART + (at_z * SIDE + low_y) * CAP
        return pl.ds(pl.multiple_of(start, CAP), count)

    def block(k, g, other, dz):
        half = 1 - half_y if other else half_y
        return rows.at[spot(k, g, 2 * half, turn(z, dz), PAIR)]

    def settle(ref, sem):
        pltpu.make_async_copy(ref, ref, sem).wait()

    def drain(ref, count, sem):
        settle(ref.at[pl.ds(0, count)], sem)

    def push(src, dst, send, recv, device):
        pltpu.make_async_remote_copy(
            src_ref=src, dst_ref=dst, send_sem=send, recv_sem=recv,
            device_id=device, device_id_type=MESH,
        ).start()

    barrier = pltpu.get_barrier_semaphore()
    partners = [sibling, across, above, below, trade]
    for step in range(SIDE):
        for mate in (False, True):
            if step or mate:
                partners.append(peer(mate, step))
    for partner in partners:
        pl.semaphore_signal(barrier, inc=1, device_id=partner, device_id_type=MESH)

    @pl.when(jnp.logical_not(guest))
    def _():
        pltpu.make_async_copy(w_in.at[0], w1, weight_recv.at[0]).start()
        pltpu.make_async_copy(w_out.at[0], w2, weight_recv.at[1]).start()

    limits = counts[...].astype(F32)
    expert_lanes = lax.broadcasted_iota(jnp.int32, (ids.shape[1], EXPERTS), 1)
    slot_lanes = lax.broadcasted_iota(jnp.int32, (ids.shape[1], EXPERTS * CAP), 1)
    picks, weighted = None, None
    ids_down, slots_down, gates_down = (
        jnp.concatenate([ref[...].astype(F32)] * 4, axis=0).T for ref in (ids, slots, gates)
    )
    for choice in range(2):
        expert = ids_down[:, choice : choice + 1].astype(jnp.int32)
        slot = slots_down[:, choice : choice + 1].astype(jnp.int32)
        limit = jnp.sum(
            jnp.where(expert == expert_lanes, limits, 0.0), axis=1, keepdims=True
        )
        place = jnp.where(slot.astype(F32) < limit, expert * CAP + slot, -1)
        pick = jnp.where(place == slot_lanes, 1.0, 0.0)
        scale = pick * gates_down[:, choice : choice + 1]
        picks = pick if picks is None else picks + pick
        weighted = scale if weighted is None else weighted + scale
    held[...] = picks.astype(BF16)
    to_slots = picks.T.astype(BF16)
    slot_gate = jnp.sum(weighted.T, axis=1, keepdims=True)
    out_x[...] = jnp.dot(to_slots, tokens[...], preferred_element_type=F32).astype(BF16)
    out_g[...] = (
        slot_gate * jnp.dot(to_slots, grad_out[...], preferred_element_type=F32)
    ).astype(BF16)
    def slots_of(expert):
        return pl.ds(pl.multiple_of(expert * CAP, CAP), CAP)

    served = x * CORES + side
    for g, source in enumerate((out_x, out_g)):
        rows[spot(0, g, y, z, CAP), :] = source[slots_of(served), :]

    pl.semaphore_wait(barrier, len(partners))

    def swap(k, mate):
        target = peer(mate, SIDE - DX[k])
        there = turn(x, SIDE - DX[k]) * CORES + (1 - side if mate else side)
        for g, source in enumerate((out_x, out_g)):
            push(
                source.at[slots_of(there)], rows.at[spot(k, g, y, z, CAP)],
                swap_send, swap_recv.at[k, int(mate)], target,
            )

    def ship(k, g, other, dz, device, event):
        where = block(k, g, other, dz)
        push(where, where, gather_send.at[k], gather_recv.at[k, event], device)

    def share(k, g, other, dz):
        where = block(k, g, other, dz)
        push(where, where, core_send.at[k], core_recv.at[k], sibling)

    def gather_start(k, first=False):
        if not first:
            drain(rows, 2 * CAP, swap_recv.at[k, 0])
        drain(rows, 2 * CAP, swap_recv.at[k, 1])
        for g in range(2):
            ship(k, g, False, 0, across, 0)
            ship(k, g, False, 0, above, 1)
            ship(k, g, False, 0, below, 2)
        for g in range(2):
            share(k, g, False, 0)

    def gather_cross(k):
        drain(rows, 2 * PAIR, gather_recv.at[k, 0])
        for g in range(2):
            ship(k, g, True, 0, above, 4)
            ship(k, g, True, 0, below, 5)
        for g in range(2):
            share(k, g, True, 0)

    def gather_pass(k):
        drain(rows, 2 * PAIR, gather_recv.at[k, 1])
        ship(k, 0, False, 3, above, 3)
        drain(rows, 2 * PAIR, gather_recv.at[k, 2])
        ship(k, 1, False, 1, below, 3)
        for g in range(2):
            share(k, g, False, 3)
            share(k, g, False, 1)

    def gather_far(k):
        drain(rows, 2 * PAIR, gather_recv.at[k, 3])
        for g in range(2):
            ship(k, g, False, 2, across, 6)
        for g in range(2):
            share(k, g, False, 2)

    def gather_end(k):
        for event, dz in ((4, 3), (5, 1), (6, 2)):
            drain(rows, 2 * PAIR, gather_recv.at[k, event])
            for g in range(2):
                share(k, g, True, dz)

    def gather_done(k):
        drain(rows, 2 * PART, core_recv.at[k])

    def section(k, g, part):
        start = ((k * 2 + g) * 2 + part) * PART
        return pl.ds(pl.multiple_of(start, PART), PART)

    def span_of(k, part):
        return pl.ds(pl.multiple_of(k * CHUNK + part * PART, PART), PART)

    def activate(k, part):
        pre = jnp.dot(rows[section(k, 0, part), :], w1[...], preferred_element_type=F32)
        activated, slope = gelu_parts(pre)
        hidden_t[:, span_of(k, part)] = activated.T.astype(BF16)
        slopes[span_of(k, part), :] = slope

    def backward(k, part):
        span = span_of(k, part)
        back_hidden = lax.dot_general(
            rows[section(k, 1, part), :], w2[...], (((1,), (1,)), ((), ())),
            preferred_element_type=F32,
        )
        change = back_hidden * slopes[span, :]
        delta[span, :] = change.astype(BF16)
        delta_t[:, span] = change.T.astype(BF16)

    def both(step, k):
        for part in range(CORES):
            step(k, part)

    def to_inputs(k, part):
        span = span_of(k, part)
        for start in range(0, width, units):
            back[span, start : start + units] = lax.dot_general(
                delta[span, :], w1[start : start + units, :], (((1,), (1,)), ((), ())),
                preferred_element_type=F32,
            ).astype(BF16)

    def product(left, g, start):
        total = None
        for k in range(CHUNKS):
            term = jnp.dot(
                left[:, k * CHUNK : (k + 1) * CHUNK],
                rows[pl.ds((k * 2 + g) * CHUNK, CHUNK), start : start + units],
                preferred_element_type=F32,
            )
            total = term if total is None else total + term
        return total

    def settle_grad(ref, target, index):
        @pl.when(guest)
        def _():
            push(ref, target, grad_send.at[index], grad_recv.at[index], trade)

        @pl.when(jnp.logical_not(guest))
        def _():
            pltpu.make_async_copy(ref, target, grad_recv.at[index]).start()

    def second_weights(index):
        columns = pl.ds(index * tile, tile)
        rounded[:, columns] = product(hidden_t, 1, index * tile).astype(BF16)
        settle_grad(rounded.at[:, columns], grad_second.at[:, columns], 0)

    def first_weights(index):
        span = pl.ds(index * tile, tile)
        turned[span, :] = product(delta_t, 0, index * tile).T.astype(BF16)
        settle_grad(turned.at[span], grad_in.at[span], 1)

    def add_start(k):
        to_inputs(k, 1 - core)
        push(
            back.at[span_of(k, 1 - core)], other_core.at[k],
            add_send.at[k], add_recv.at[k], sibling,
        )
        to_inputs(k, core)

    def lump(k, other, dz, first=0, count=PAIR):
        half = 1 - half_y if other else half_y
        start = k * CHUNK + core * PART + (turn(z, dz) * SIDE + 2 * half) * CAP + first
        return pl.ds(pl.multiple_of(start, CAP), count)

    def add(where, *terms):
        total = back[where, :].astype(F32)
        for term in terms:
            total = total + term.astype(F32)
        back[where, :] = total.astype(BF16)

    def forward(k, where, target, event, device):
        push(back.at[where], target, sum_send.at[k], sum_recv.at[k, event], device)

    def sum_start(k):
        settle(other_core.at[k], add_recv.at[k])
        add(span_of(k, core), other_core[k])
        forward(k, lump(k, True, 2), sum_a.at[k], 0, across)
        forward(k, lump(k, True, 1), sum_b.at[k, 0], 1, above)
        forward(k, lump(k, True, 3), sum_b.at[k, 1], 2, below)
        forward(k, lump(k, False, 1, CAP, CAP), sum_e.at[k, 0, pl.ds(CAP, CAP)], 6, above)
        forward(k, lump(k, False, 3, 0, CAP), sum_e.at[k, 1, pl.ds(0, CAP)], 7, below)

    def sum_far(k):
        settle(sum_a.at[k], sum_recv.at[k, 0])
        add(lump(k, False, 2), sum_a[k])
        forward(k, lump(k, False, 2, 0, CAP), sum_c.at[k, 0], 3, above)
        forward(k, lump(k, False, 2, CAP, CAP), sum_c.at[k, 1], 4, below)

    def sum_cross(k):
        settle(sum_b.at[k, 0], sum_recv.at[k, 1])
        settle(sum_b.at[k, 1], sum_recv.at[k, 2])
        add(lump(k, True, 0), sum_b[k, 0], sum_b[k, 1])
        forward(k, lump(k, True, 0), sum_d.at[k], 5, across)

    def sum_pass(k):
        settle(sum_c.at[k, 0], sum_recv.at[k, 3])
        add(lump(k, False, 1, 0, CAP), sum_c[k, 0])
        forward(k, lump(k, False, 1, 0, CAP), sum_e.at[k, 0, pl.ds(0, CAP)], 6, above)
        settle(sum_c.at[k, 1], sum_recv.at[k, 4])
        add(lump(k, False, 3, CAP, CAP), sum_c[k, 1])
        forward(k, lump(k, False, 3, CAP, CAP), sum_e.at[k, 1, pl.ds(CAP, CAP)], 7, below)

    def sum_end(k):
        settle(sum_d.at[k], sum_recv.at[k, 5])
        settle(sum_e.at[k, 0], sum_recv.at[k, 6])
        settle(sum_e.at[k, 1], sum_recv.at[k, 7])
        final[k] = (
            back[lump(k, False, 0), :].astype(F32) + sum_d[k].astype(F32)
            + sum_e[k, 0].astype(F32) + sum_e[k, 1].astype(F32)
        ).astype(BF16)
        mine = pl.ds(pl.multiple_of((y - 2 * half_y) * CAP, CAP), CAP)
        mates = pl.ds(pl.multiple_of((mate_y - 2 * half_y) * CAP, CAP), CAP)
        if k == 0:
            returned[slots_of(served), :] = final[k, mine, :]
        else:
            push(
                final.at[k, mine], returned.at[slots_of(served)],
                home_send, home_recv.at[k, 0], peer(False, DX[k]),
            )
        push(
            final.at[k, mates], returned.at[slots_of(served)],
            home_send, home_recv.at[k, 1], peer(True, DX[k]),
        )

    swap(0, True)
    gather_start(0, first=True)
    swap(1, True)
    swap(1, False)

    @pl.when(guest)
    def _():
        push(w_in.at[0], w1, weight_send.at[0], weight_recv.at[0], trade)
        push(w_out.at[0], w2, weight_send.at[1], weight_recv.at[1], trade)

    gather_pass(0)
    gather_cross(0)
    gather_start(1)
    swap(2, True)
    swap(2, False)
    gather_far(0)
    swap(3, True)
    swap(3, False)
    gather_start(2)
    gather_pass(1)
    gather_cross(1)
    gather_far(1)
    gather_end(0)
    gather_start(3)
    gather_pass(2)
    gather_cross(2)
    gather_far(2)
    gather_end(1)
    first = pltpu.make_async_copy(held, picked_out, store_sem.at[0])
    first.start()
    settle(w1, weight_recv.at[0])
    gather_done(0)
    both(activate, 0)
    gather_pass(3)
    gather_cross(3)
    gather_done(1)
    both(activate, 1)
    gather_far(3)
    gather_end(2)
    gather_done(2)
    both(activate, 2)
    settle(w2, weight_recv.at[1])
    both(backward, 0)
    both(backward, 1)
    gather_end(3)
    both(backward, 2)
    gather_done(3)
    both(activate, 3)
    both(backward, 3)
    second_weights(0)
    add_start(0)
    second_weights(1)
    sum_start(0)
    add_start(1)
    second_weights(2)
    sum_far(0)
    sum_cross(0)
    sum_start(1)
    add_start(2)
    second_weights(3)
    sum_pass(0)
    sum_far(1)
    sum_cross(1)
    first_weights(0)
    sum_start(2)
    add_start(3)
    sum_end(0)
    first_weights(1)
    sum_pass(1)
    sum_far(2)
    sum_cross(2)
    first_weights(2)
    sum_start(3)
    sum_end(1)
    first_weights(3)
    sum_pass(2)
    sum_far(3)
    sum_cross(3)
    sum_end(2)
    sum_pass(3)
    sum_end(3)

    for k in range(CHUNKS):
        if k:
            drain(returned, CAP, home_recv.at[k, 0])
        drain(returned, CAP, home_recv.at[k, 1])
    last = pltpu.make_async_copy(returned, returned_out, store_sem.at[1])
    last.start()
    settle(grad_second, grad_recv.at[0])
    settle(grad_in, grad_recv.at[1])

    @pl.when(guest)
    def _():
        settle(w1, weight_send.at[0])
        settle(w2, weight_send.at[1])
        settle(grad_second, grad_send.at[0])
        settle(grad_in, grad_send.at[1])

    drain(rows, 2 * (2 * SIDE - 1) * CAP, swap_send)
    drain(rows, (2 * SIDE - 1) * CAP, home_send)
    for k in range(CHUNKS):
        drain(rows, 14 * PAIR, gather_send.at[k])
        drain(rows, 2 * PART, core_send.at[k])
        drain(rows, PART, add_send.at[k])
        drain(rows, 7 * PAIR, sum_send.at[k])
    first.wait()
    last.wait()


def finish(
    picked, returned, turned, rounded,
    grad_tokens, grad_in, grad_second,
    from_first, from_second, to_first, to_second, rows, held, total, load_sem, store_sem,
):
    loads, stores = [], []
    for source, near in ((picked, held), (returned, rows)):
        loads.append(pltpu.make_async_copy(source, near, load_sem.at[len(loads)]))
    for source, near in ((turned, from_first), (rounded, from_second)):
        height = source.shape[0] // PIECES
        for piece in range(PIECES):
            span = pl.ds(piece * height, height)
            loads.append(
                pltpu.make_async_copy(source.at[span], near.at[span], load_sem.at[len(loads)])
            )
    for load in loads:
        load.start()

    def store(near, target):
        stores.append(pltpu.make_async_copy(near, target, store_sem.at[len(stores)]))
        stores[-1].start()

    for load in loads[:2]:
        load.wait()
    total[...] = jnp.dot(held[...], rows[...], preferred_element_type=F32).astype(BF16)
    store(total, grad_tokens)
    arrivals = iter(loads[2:])
    for near, wide, target in (
        (from_first, to_first, grad_in), (from_second, to_second, grad_second),
    ):
        height = near.shape[0] // PIECES
        for piece in range(PIECES):
            span = pl.ds(piece * height, height)
            next(arrivals).wait()
            wide[span, :] = near[span, :].astype(F32)
            store(wide.at[span], target.at[0, span])
    for started in stores:
        started.wait()


def body(tokens, grad_out, gate_weights, expert_ids, slot_ids, counts, w_in, w_out):
    token_rows, width = tokens.shape
    units = w_out.shape[1]
    in_vmem = pl.BlockSpec(memory_space=pltpu.VMEM)
    in_hbm = pl.BlockSpec(memory_space=pl.ANY)
    dma = pltpu.SemaphoreType.DMA
    slots = EXPERTS * CAP
    results = pl.pallas_call(
        kernel,
        out_shape=(
            jax.ShapeDtypeStruct((token_rows, slots), BF16),
            jax.ShapeDtypeStruct((slots, width), BF16),
            jax.ShapeDtypeStruct((width, units), BF16),
            jax.ShapeDtypeStruct((units, width), BF16),
        ),
        in_specs=[in_vmem] * 6 + [in_hbm] * 2,
        out_specs=(in_hbm,) * 4,
        scratch_shapes=[
            pltpu.VMEM((CHUNKS * 2 * CHUNK, width), BF16),
            pltpu.VMEM((width, units), BF16),
            pltpu.VMEM((units, width), BF16),
            pltpu.VMEM((CHUNKS * CHUNK, width), BF16),
            pltpu.VMEM((CHUNKS, PART, width), BF16),
            pltpu.VMEM((width, units), BF16),
            pltpu.VMEM((units, width), BF16),
            pltpu.VMEM((EXPERTS * CAP, width), BF16),
            pltpu.VMEM((EXPERTS * CAP, width), BF16),
            pltpu.VMEM((EXPERTS * CAP, width), BF16),
            pltpu.VMEM((token_rows, EXPERTS * CAP), BF16),
            pltpu.VMEM((units, CHUNKS * CHUNK), BF16),
            pltpu.VMEM((CHUNKS * CHUNK, units), BF16),
            pltpu.VMEM((units, CHUNKS * CHUNK), BF16),
            pltpu.VMEM((CHUNKS * CHUNK, units), F32),
            pltpu.VMEM((CHUNKS, PAIR, width), BF16),
            pltpu.VMEM((CHUNKS, 2, PAIR, width), BF16),
            pltpu.VMEM((CHUNKS, 2, CAP, width), BF16),
            pltpu.VMEM((CHUNKS, PAIR, width), BF16),
            pltpu.VMEM((CHUNKS, 2, PAIR, width), BF16),
            pltpu.VMEM((CHUNKS, PAIR, width), BF16),
            dma((2,)),
            dma((2,)),
            dma((2,)),
            dma,
            dma((CHUNKS, 2)),
            dma((CHUNKS,)),
            dma((CHUNKS, 7)),
            dma((CHUNKS,)),
            dma((CHUNKS,)),
            dma((CHUNKS,)),
            dma((CHUNKS,)),
            dma((CHUNKS,)),
            dma((CHUNKS, 8)),
            dma((2,)),
            dma((2,)),
            dma,
            dma((CHUNKS, 2)),
        ],
        compiler_params=pltpu.CompilerParams(
            collective_id=0, has_side_effects=True, vmem_limit_bytes=62 * 2**20
        ),
        cost_estimate=pl.CostEstimate(
            flops=10 * NODES * EXPERTS * CAP * width * units,
            bytes_accessed=16 * width * units,
            transcendentals=0,
        ),
    )(tokens, grad_out, gate_weights.T, expert_ids.T, slot_ids.T, counts, w_in, w_out)
    return pl.pallas_call(
        finish,
        out_shape=(
            jax.ShapeDtypeStruct(tokens.shape, BF16),
            jax.ShapeDtypeStruct(w_in.shape, F32),
            jax.ShapeDtypeStruct(w_out.shape, F32),
        ),
        in_specs=[in_hbm] * 4,
        out_specs=(in_hbm,) * 3,
        scratch_shapes=[
            pltpu.VMEM((width, units), BF16),
            pltpu.VMEM((units, width), BF16),
            pltpu.VMEM((width, units), F32),
            pltpu.VMEM((units, width), F32),
            pltpu.VMEM((slots, width), BF16),
            pltpu.VMEM((token_rows, slots), BF16),
            pltpu.VMEM((token_rows, width), BF16),
            dma((2 + 2 * PIECES,)),
            dma((1 + 2 * PIECES,)),
        ],
        compiler_params=pltpu.CompilerParams(vmem_limit_bytes=62 * 2**20),
    )(*results)


def solution(mesh):
    placed = (
        P(("node", "local"), None),
        P(("node", "local"), None),
        P(("node", "local"), None),
        P(("node", "local"), None),
        P(("node", "local"), None),
        P(("node", "local"), None),
        P("local", None, "node"),
        P("local", "node", None),
    )
    return jax.shard_map(
        body,
        mesh=mesh,
        in_specs=placed,
        out_specs=(P(("node", "local"), None), P("local", None, "node"), P("local", "node", None)),
        check_vma=False,
    )
```

```python
import functools

import jax
import jax.numpy as jnp
from jax import lax
from jax.experimental import pallas as pl
from jax.experimental.pallas import tpu as pltpu
from jax.sharding import PartitionSpec as P

MESH = pl.DeviceIdType.MESH
BF16 = jnp.bfloat16
F32 = jnp.float32

SIDE = 4
CORES = 2
EXPERTS = 8
CAP = 16
NODES = SIDE * SIDE
CHUNKS = SIDE
DX = (0, 1, 3, 2)
PAIR = 2 * CAP
PART = NODES * CAP
CHUNK = CORES * PART
PIECES = 4
TILES = 4


def gelu_parts(values):
    cumulative = 0.5 * (1.0 + lax.erf(values * 0.7071067811865476))
    density = values * jnp.exp(-0.5 * values * values) * 0.3989422804014327
    return (values * cumulative, cumulative + density)


def turn(value, step):
    return lax.rem(value + step, SIDE)


def kernel(
    tokens, grad_out, gates, ids, slots, counts, w_in, w_out,
    picked_out, returned_out, grad_in, grad_second,
    rows, w1, w2, back, other_core, turned, rounded, out_x, out_g, returned, held,
    hidden_t, delta, delta_t, slopes, sum_a, sum_b, sum_c, sum_d, sum_e, final,
    weight_send, weight_recv, store_sem, swap_send, swap_recv,
    gather_send, gather_recv, core_send, core_recv,
    add_send, add_recv, sum_send, sum_recv, grad_send, grad_recv, home_send, home_recv,
):
    width = rows.shape[1]
    units = w2.shape[0]
    tile = width // TILES
    node, local = lax.axis_index("node"), lax.axis_index("local")
    y, z = node // SIDE, lax.rem(node, SIDE)
    x, core = local // CORES, lax.rem(local, CORES)

    side = lax.rem((y + 1) // 2, 2)
    half_y = y // 2
    mate_y = y + 1 - 2 * lax.rem(y, 2)
    guest = core != side

    def turn(value, step):
        return lax.rem(value + step, SIDE)

    sibling = (node, x * CORES + 1 - core)
    across = ((SIDE - 1 - y) * SIDE + z, local)
    above = (y * SIDE + turn(z, 1), local)
    below = (y * SIDE + turn(z, 3), local)
    trade = (mate_y * SIDE + z, x * CORES + 1 - core)

    def peer(mate, step):
        there = mate_y if mate else y
        return (there * SIDE + z, turn(x, step) * CORES + core)

    def spot(k, g, low_y, at_z, count):
        start = ((k * 2 + g) * 2 + core) * PART + (at_z * SIDE + low_y) * CAP
        return pl.ds(pl.multiple_of(start, CAP), count)

    def block(k, g, other, dz):
        half = 1 - half_y if other else half_y
        return rows.at[spot(k, g, 2 * half, turn(z, dz), PAIR)]

    def settle(ref, sem):
        pltpu.make_async_copy(ref, ref, sem).wait()

    def drain(ref, count, sem):
        settle(ref.at[pl.ds(0, count)], sem)

    def push(src, dst, send, recv, device):
        pltpu.make_async_remote_copy(
            src_ref=src, dst_ref=dst, send_sem=send, recv_sem=recv,
            device_id=device, device_id_type=MESH,
        ).start()

    barrier = pltpu.get_barrier_semaphore()
    partners = [sibling, across, above, below, trade]
    for step in range(SIDE):
        for mate in (False, True):
            if step or mate:
                partners.append(peer(mate, step))
    for partner in partners:
        pl.semaphore_signal(barrier, inc=1, device_id=partner, device_id_type=MESH)

    @pl.when(jnp.logical_not(guest))
    def _():
        pltpu.make_async_copy(w_in.at[0], w1, weight_recv.at[0]).start()
        pltpu.make_async_copy(w_out.at[0], w2, weight_recv.at[1]).start()

    limits = counts[...].astype(F32)
    expert_lanes = lax.broadcasted_iota(jnp.int32, (ids.shape[1], EXPERTS), 1)
    slot_lanes = lax.broadcasted_iota(jnp.int32, (ids.shape[1], EXPERTS * CAP), 1)
    picks, weighted = None, None
    ids_down, slots_down, gates_down = (
        jnp.concatenate([ref[...].astype(F32)] * 4, axis=0).T for ref in (ids, slots, gates)
    )
    for choice in range(2):
        expert = ids_down[:, choice : choice + 1].astype(jnp.int32)
        slot = slots_down[:, choice : choice + 1].astype(jnp.int32)
        limit = jnp.sum(
            jnp.where(expert == expert_lanes, limits, 0.0), axis=1, keepdims=True
        )
        place = jnp.where(slot.astype(F32) < limit, expert * CAP + slot, -1)
        pick = jnp.where(place == slot_lanes, 1.0, 0.0)
        scale = pick * gates_down[:, choice : choice + 1]
        picks = pick if picks is None else picks + pick
        weighted = scale if weighted is None else weighted + scale
    held[...] = picks.astype(BF16)
    to_slots = picks.T.astype(BF16)
    slot_gate = jnp.sum(weighted.T, axis=1, keepdims=True)
    out_x[...] = jnp.dot(to_slots, tokens[...], preferred_element_type=F32).astype(BF16)
    out_g[...] = (
        slot_gate * jnp.dot(to_slots, grad_out[...], preferred_element_type=F32)
    ).astype(BF16)
    def slots_of(expert):
        return pl.ds(pl.multiple_of(expert * CAP, CAP), CAP)

    served = x * CORES + side
    for g, source in enumerate((out_x, out_g)):
        rows[spot(0, g, y, z, CAP), :] = source[slots_of(served), :]

    pl.semaphore_wait(barrier, len(partners))

    def swap(k, mate):
        target = peer(mate, SIDE - DX[k])
        there = turn(x, SIDE - DX[k]) * CORES + (1 - side if mate else side)
        for g, source in enumerate((out_x, out_g)):
            push(
                source.at[slots_of(there)], rows.at[spot(k, g, y, z, CAP)],
                swap_send, swap_recv.at[k, int(mate)], target,
            )

    def ship(k, g, other, dz, device, event):
        where = block(k, g, other, dz)
        push(where, where, gather_send.at[k], gather_recv.at[k, event], device)

    def share(k, g, other, dz):
        where = block(k, g, other, dz)
        push(where, where, core_send.at[k], core_recv.at[k], sibling)

    def gather_first(from_y):
        for g in range(2):
            where = rows.at[spot(0, g, from_y, z, CAP)]
            for event, device in enumerate((across, above, below)):
                push(where, where, gather_send.at[0], gather_recv.at[0, event], device)
        for g in range(2):
            where = rows.at[spot(0, g, from_y, z, CAP)]
            push(where, where, core_send.at[0], core_recv.at[0], sibling)

    def gather_start(k):
        for mate in range(2):
            drain(rows, 2 * CAP, swap_recv.at[k, mate])
        for g in range(2):
            ship(k, g, False, 0, across, 0)
            ship(k, g, False, 0, above, 1)
            ship(k, g, False, 0, below, 2)
        for g in range(2):
            share(k, g, False, 0)

    def gather_mate():
        drain(rows, 2 * CAP, swap_recv.at[0, 1])
        gather_first(mate_y)

    def gather_cross(k):
        drain(rows, 2 * PAIR, gather_recv.at[k, 0])
        for g in range(2):
            ship(k, g, True, 0, above, 4)
            ship(k, g, True, 0, below, 5)
        for g in range(2):
            share(k, g, True, 0)

    def gather_pass(k):
        drain(rows, 2 * PAIR, gather_recv.at[k, 1])
        ship(k, 0, False, 3, above, 3)
        drain(rows, 2 * PAIR, gather_recv.at[k, 2])
        ship(k, 1, False, 1, below, 3)
        for g in range(2):
            share(k, g, False, 3)
            share(k, g, False, 1)

    def gather_far(k):
        drain(rows, 2 * PAIR, gather_recv.at[k, 3])
        for g in range(2):
            ship(k, g, False, 2, across, 6)
        for g in range(2):
            share(k, g, False, 2)

    def gather_end(k):
        for event, dz in ((4, 3), (5, 1), (6, 2)):
            drain(rows, 2 * PAIR, gather_recv.at[k, event])
            for g in range(2):
                share(k, g, True, dz)

    def gather_done(k):
        drain(rows, 2 * PART, core_recv.at[k])

    def section(k, g, part):
        start = ((k * 2 + g) * 2 + part) * PART
        return pl.ds(pl.multiple_of(start, PART), PART)

    def span_of(k, part):
        return pl.ds(pl.multiple_of(k * CHUNK + part * PART, PART), PART)

    def activate(k, part):
        pre = jnp.dot(rows[section(k, 0, part), :], w1[...], preferred_element_type=F32)
        activated, slope = gelu_parts(pre)
        hidden_t[:, span_of(k, part)] = activated.T.astype(BF16)
        slopes[span_of(k, part), :] = slope

    def backward(k, part):
        span = span_of(k, part)
        back_hidden = lax.dot_general(
            rows[section(k, 1, part), :], w2[...], (((1,), (1,)), ((), ())),
            preferred_element_type=F32,
        )
        change = back_hidden * slopes[span, :]
        delta[span, :] = change.astype(BF16)
        delta_t[:, span] = change.T.astype(BF16)

    def both(step, k):
        for part in range(CORES):
            step(k, part)

    def slopes_of(k, part):
        activate(k, part)
        backward(k, part)

    def to_inputs(k, part):
        span = span_of(k, part)
        for start in range(0, width, units):
            back[span, start : start + units] = lax.dot_general(
                delta[span, :], w1[start : start + units, :], (((1,), (1,)), ((), ())),
                preferred_element_type=F32,
            ).astype(BF16)

    def product(left, g, start):
        total = None
        for k in range(CHUNKS):
            term = jnp.dot(
                left[:, k * CHUNK : (k + 1) * CHUNK],
                rows[pl.ds((k * 2 + g) * CHUNK, CHUNK), start : start + units],
                preferred_element_type=F32,
            )
            total = term if total is None else total + term
        return total

    def settle_grad(ref, target, index):
        @pl.when(guest)
        def _():
            push(ref, target, grad_send.at[index], grad_recv.at[index], trade)

        @pl.when(jnp.logical_not(guest))
        def _():
            pltpu.make_async_copy(ref, target, grad_recv.at[index]).start()

    def second_weights(index):
        columns = pl.ds(index * tile, tile)
        rounded[:, columns] = product(hidden_t, 1, index * tile).astype(BF16)
        settle_grad(rounded.at[:, columns], grad_second.at[:, columns], 0)

    def first_weights(index):
        span = pl.ds(index * tile, tile)
        turned[span, :] = product(delta_t, 0, index * tile).T.astype(BF16)
        settle_grad(turned.at[span], grad_in.at[span], 1)

    def add_start(k):
        to_inputs(k, 1 - core)
        push(
            back.at[span_of(k, 1 - core)], other_core.at[k],
            add_send.at[k], add_recv.at[k], sibling,
        )
        to_inputs(k, core)

    def lump(k, other, dz, first=0, count=PAIR):
        half = 1 - half_y if other else half_y
        start = k * CHUNK + core * PART + (turn(z, dz) * SIDE + 2 * half) * CAP + first
        return pl.ds(pl.multiple_of(start, CAP), count)

    def add(where, *terms):
        total = back[where, :].astype(F32)
        for term in terms:
            total = total + term.astype(F32)
        back[where, :] = total.astype(BF16)

    def forward(k, where, target, event, device):
        push(back.at[where], target, sum_send.at[k], sum_recv.at[k, event], device)

    def sum_start(k):
        settle(other_core.at[k], add_recv.at[k])
        add(span_of(k, core), other_core[k])
        forward(k, lump(k, True, 2), sum_a.at[k], 0, across)
        forward(k, lump(k, True, 1), sum_b.at[k, 0], 1, above)
        forward(k, lump(k, True, 3), sum_b.at[k, 1], 2, below)
        forward(k, lump(k, False, 1, CAP, CAP), sum_e.at[k, 0, pl.ds(CAP, CAP)], 6, above)
        forward(k, lump(k, False, 3, 0, CAP), sum_e.at[k, 1, pl.ds(0, CAP)], 7, below)

    def sum_far(k):
        settle(sum_a.at[k], sum_recv.at[k, 0])
        add(lump(k, False, 2), sum_a[k])
        forward(k, lump(k, False, 2, 0, CAP), sum_c.at[k, 0], 3, above)
        forward(k, lump(k, False, 2, CAP, CAP), sum_c.at[k, 1], 4, below)

    def sum_cross(k):
        settle(sum_b.at[k, 0], sum_recv.at[k, 1])
        settle(sum_b.at[k, 1], sum_recv.at[k, 2])
        add(lump(k, True, 0), sum_b[k, 0], sum_b[k, 1])
        forward(k, lump(k, True, 0), sum_d.at[k], 5, across)

    def sum_pass(k):
        settle(sum_c.at[k, 0], sum_recv.at[k, 3])
        add(lump(k, False, 1, 0, CAP), sum_c[k, 0])
        forward(k, lump(k, False, 1, 0, CAP), sum_e.at[k, 0, pl.ds(0, CAP)], 6, above)
        settle(sum_c.at[k, 1], sum_recv.at[k, 4])
        add(lump(k, False, 3, CAP, CAP), sum_c[k, 1])
        forward(k, lump(k, False, 3, CAP, CAP), sum_e.at[k, 1, pl.ds(CAP, CAP)], 7, below)

    def sum_end(k):
        settle(sum_d.at[k], sum_recv.at[k, 5])
        settle(sum_e.at[k, 0], sum_recv.at[k, 6])
        settle(sum_e.at[k, 1], sum_recv.at[k, 7])
        final[k] = (
            back[lump(k, False, 0), :].astype(F32) + sum_d[k].astype(F32)
            + sum_e[k, 0].astype(F32) + sum_e[k, 1].astype(F32)
        ).astype(BF16)
        mine = pl.ds(pl.multiple_of((y - 2 * half_y) * CAP, CAP), CAP)
        mates = pl.ds(pl.multiple_of((mate_y - 2 * half_y) * CAP, CAP), CAP)
        if k == 0:
            returned[slots_of(served), :] = final[k, mine, :]
        else:
            push(
                final.at[k, mine], returned.at[slots_of(served)],
                home_send, home_recv.at[k, 0], peer(False, DX[k]),
            )
        push(
            final.at[k, mates], returned.at[slots_of(served)],
            home_send, home_recv.at[k, 1], peer(True, DX[k]),
        )

    swap(0, True)
    gather_first(y)
    gather_mate()
    swap(1, True)
    swap(1, False)

    @pl.when(guest)
    def _():
        push(w_in.at[0], w1, weight_send.at[0], weight_recv.at[0], trade)
        push(w_out.at[0], w2, weight_send.at[1], weight_recv.at[1], trade)

    gather_pass(0)
    gather_cross(0)
    gather_start(1)
    swap(2, True)
    swap(2, False)
    gather_far(0)
    swap(3, True)
    swap(3, False)
    gather_start(2)
    gather_pass(1)
    gather_cross(1)
    gather_start(3)
    gather_far(1)
    gather_end(0)
    gather_pass(2)
    gather_cross(2)
    gather_far(2)
    gather_end(1)
    first = pltpu.make_async_copy(held, picked_out, store_sem.at[0])
    first.start()
    settle(w1, weight_recv.at[0])
    gather_done(0)
    both(activate, 0)
    gather_pass(3)
    gather_cross(3)
    gather_done(1)
    both(activate, 1)
    gather_far(3)
    gather_end(2)
    gather_done(2)
    both(activate, 2)
    settle(w2, weight_recv.at[1])
    both(backward, 0)
    both(backward, 1)
    both(backward, 2)
    gather_end(3)
    slopes_of(3, core)
    gather_done(3)
    slopes_of(3, 1 - core)
    second_weights(0)
    add_start(0)
    second_weights(1)
    sum_start(0)
    add_start(1)
    second_weights(2)
    sum_far(0)
    sum_cross(0)
    sum_start(1)
    add_start(2)
    second_weights(3)
    first_weights(0)
    sum_pass(0)
    sum_far(1)
    sum_cross(1)
    sum_start(2)
    add_start(3)
    first_weights(1)
    sum_end(0)
    sum_pass(1)
    sum_far(2)
    sum_cross(2)
    first_weights(2)
    sum_start(3)
    first_weights(3)
    sum_end(1)
    sum_pass(2)
    sum_far(3)
    sum_cross(3)
    sum_end(2)
    sum_pass(3)
    sum_end(3)

    for k in range(CHUNKS):
        if k:
            drain(returned, CAP, home_recv.at[k, 0])
        drain(returned, CAP, home_recv.at[k, 1])
    last = pltpu.make_async_copy(returned, returned_out, store_sem.at[1])
    last.start()
    settle(grad_second, grad_recv.at[0])
    settle(grad_in, grad_recv.at[1])

    @pl.when(guest)
    def _():
        settle(w1, weight_send.at[0])
        settle(w2, weight_send.at[1])
        settle(grad_second, grad_send.at[0])
        settle(grad_in, grad_send.at[1])

    drain(rows, 2 * (2 * SIDE - 1) * CAP, swap_send)
    drain(rows, (2 * SIDE - 1) * CAP, home_send)
    for k in range(CHUNKS):
        drain(rows, 14 * PAIR, gather_send.at[k])
        drain(rows, 2 * PART, core_send.at[k])
        drain(rows, PART, add_send.at[k])
        drain(rows, 7 * PAIR, sum_send.at[k])
    first.wait()
    last.wait()


def finish(
    picked, returned, turned, rounded,
    grad_tokens, grad_in, grad_second,
    from_first, from_second, to_first, to_second, rows, held, total, load_sem, store_sem,
):
    loads, stores = [], []
    for source, near in ((picked, held), (returned, rows)):
        loads.append(pltpu.make_async_copy(source, near, load_sem.at[len(loads)]))
    for source, near in ((turned, from_first), (rounded, from_second)):
        height = source.shape[0] // PIECES
        for piece in range(PIECES):
            span = pl.ds(piece * height, height)
            loads.append(
                pltpu.make_async_copy(source.at[span], near.at[span], load_sem.at[len(loads)])
            )
    for load in loads:
        load.start()

    def store(near, target):
        stores.append(pltpu.make_async_copy(near, target, store_sem.at[len(stores)]))
        stores[-1].start()

    for load in loads[:2]:
        load.wait()
    total[...] = jnp.dot(held[...], rows[...], preferred_element_type=F32).astype(BF16)
    store(total, grad_tokens)
    arrivals = iter(loads[2:])
    for near, wide, target in (
        (from_first, to_first, grad_in), (from_second, to_second, grad_second),
    ):
        height = near.shape[0] // PIECES
        for piece in range(PIECES):
            span = pl.ds(piece * height, height)
            next(arrivals).wait()
            wide[span, :] = near[span, :].astype(F32)
            store(wide.at[span], target.at[0, span])
    for started in stores:
        started.wait()


def body(tokens, grad_out, gate_weights, expert_ids, slot_ids, counts, w_in, w_out):
    token_rows, width = tokens.shape
    units = w_out.shape[1]
    in_vmem = pl.BlockSpec(memory_space=pltpu.VMEM)
    in_hbm = pl.BlockSpec(memory_space=pl.ANY)
    dma = pltpu.SemaphoreType.DMA
    slots = EXPERTS * CAP
    results = pl.pallas_call(
        kernel,
        out_shape=(
            jax.ShapeDtypeStruct((token_rows, slots), BF16),
            jax.ShapeDtypeStruct((slots, width), BF16),
            jax.ShapeDtypeStruct((width, units), BF16),
            jax.ShapeDtypeStruct((units, width), BF16),
        ),
        in_specs=[in_vmem] * 6 + [in_hbm] * 2,
        out_specs=(in_hbm,) * 4,
        scratch_shapes=[
            pltpu.VMEM((CHUNKS * 2 * CHUNK, width), BF16),
            pltpu.VMEM((width, units), BF16),
            pltpu.VMEM((units, width), BF16),
            pltpu.VMEM((CHUNKS * CHUNK, width), BF16),
            pltpu.VMEM((CHUNKS, PART, width), BF16),
            pltpu.VMEM((width, units), BF16),
            pltpu.VMEM((units, width), BF16),
            pltpu.VMEM((EXPERTS * CAP, width), BF16),
            pltpu.VMEM((EXPERTS * CAP, width), BF16),
            pltpu.VMEM((EXPERTS * CAP, width), BF16),
            pltpu.VMEM((token_rows, EXPERTS * CAP), BF16),
            pltpu.VMEM((units, CHUNKS * CHUNK), BF16),
            pltpu.VMEM((CHUNKS * CHUNK, units), BF16),
            pltpu.VMEM((units, CHUNKS * CHUNK), BF16),
            pltpu.VMEM((CHUNKS * CHUNK, units), F32),
            pltpu.VMEM((CHUNKS, PAIR, width), BF16),
            pltpu.VMEM((CHUNKS, 2, PAIR, width), BF16),
            pltpu.VMEM((CHUNKS, 2, CAP, width), BF16),
            pltpu.VMEM((CHUNKS, PAIR, width), BF16),
            pltpu.VMEM((CHUNKS, 2, PAIR, width), BF16),
            pltpu.VMEM((CHUNKS, PAIR, width), BF16),
            dma((2,)),
            dma((2,)),
            dma((2,)),
            dma,
            dma((CHUNKS, 2)),
            dma((CHUNKS,)),
            dma((CHUNKS, 7)),
            dma((CHUNKS,)),
            dma((CHUNKS,)),
            dma((CHUNKS,)),
            dma((CHUNKS,)),
            dma((CHUNKS,)),
            dma((CHUNKS, 8)),
            dma((2,)),
            dma((2,)),
            dma,
            dma((CHUNKS, 2)),
        ],
        compiler_params=pltpu.CompilerParams(
            collective_id=0, has_side_effects=True, vmem_limit_bytes=62 * 2**20
        ),
        cost_estimate=pl.CostEstimate(
            flops=10 * NODES * EXPERTS * CAP * width * units,
            bytes_accessed=16 * width * units,
            transcendentals=0,
        ),
    )(tokens, grad_out, gate_weights.T, expert_ids.T, slot_ids.T, counts, w_in, w_out)
    return pl.pallas_call(
        finish,
        out_shape=(
            jax.ShapeDtypeStruct(tokens.shape, BF16),
            jax.ShapeDtypeStruct(w_in.shape, F32),
            jax.ShapeDtypeStruct(w_out.shape, F32),
        ),
        in_specs=[in_hbm] * 4,
        out_specs=(in_hbm,) * 3,
        scratch_shapes=[
            pltpu.VMEM((width, units), BF16),
            pltpu.VMEM((units, width), BF16),
            pltpu.VMEM((width, units), F32),
            pltpu.VMEM((units, width), F32),
            pltpu.VMEM((slots, width), BF16),
            pltpu.VMEM((token_rows, slots), BF16),
            pltpu.VMEM((token_rows, width), BF16),
            dma((2 + 2 * PIECES,)),
            dma((1 + 2 * PIECES,)),
        ],
        compiler_params=pltpu.CompilerParams(vmem_limit_bytes=62 * 2**20),
    )(*results)


def solution(mesh):
    placed = (
        P(("node", "local"), None),
        P(("node", "local"), None),
        P(("node", "local"), None),
        P(("node", "local"), None),
        P(("node", "local"), None),
        P(("node", "local"), None),
        P("local", None, "node"),
        P("local", "node", None),
    )
    return jax.shard_map(
        body,
        mesh=mesh,
        in_specs=placed,
        out_specs=(P(("node", "local"), None), P("local", None, "node"), P("local", "node", None)),
        check_vma=False,
    )
```

```python
import functools

import jax
import jax.numpy as jnp
from jax import lax
from jax.experimental import pallas as pl
from jax.experimental.pallas import tpu as pltpu
from jax.sharding import PartitionSpec as P

MESH = pl.DeviceIdType.MESH
BF16 = jnp.bfloat16
F32 = jnp.float32

SIDE = 4
CORES = 2
EXPERTS = 8
CAP = 16
NODES = SIDE * SIDE
CHUNKS = SIDE
DX = (0, 1, 3, 2)
PAIR = 2 * CAP
PART = NODES * CAP
CHUNK = CORES * PART
PIECES = 4
TILES = 4


def gelu_parts(values):
    cumulative = 0.5 * (1.0 + lax.erf(values * 0.7071067811865476))
    density = values * jnp.exp(-0.5 * values * values) * 0.3989422804014327
    return (values * cumulative, cumulative + density)


def turn(value, step):
    return lax.rem(value + step, SIDE)


def kernel(
    tokens, grad_out, gates, ids, slots, counts, w_in, w_out,
    picked_out, returned_out, grad_in, grad_second,
    rows, w1, w2, back, other_core, turned, rounded, out_x, out_g, returned, held,
    hidden_t, delta, delta_t, slopes, sum_a, sum_b, sum_c, sum_d, sum_e, final, early,
    weight_send, weight_recv, store_sem, swap_send, swap_recv,
    gather_send, gather_recv, core_send, core_recv,
    add_send, add_recv, sum_send, sum_recv, grad_send, grad_recv, home_send, home_recv,
):
    width = rows.shape[1]
    units = w2.shape[0]
    tile = width // TILES
    node, local = lax.axis_index("node"), lax.axis_index("local")
    y, z = node // SIDE, lax.rem(node, SIDE)
    x, core = local // CORES, lax.rem(local, CORES)

    side = lax.rem((y + 1) // 2, 2)
    half_y = y // 2
    mate_y = y + 1 - 2 * lax.rem(y, 2)
    guest = core != side

    def turn(value, step):
        return lax.rem(value + step, SIDE)

    sibling = (node, x * CORES + 1 - core)
    across = ((SIDE - 1 - y) * SIDE + z, local)
    above = (y * SIDE + turn(z, 1), local)
    below = (y * SIDE + turn(z, 3), local)
    trade = (mate_y * SIDE + z, x * CORES + 1 - core)

    def peer(mate, step):
        there = mate_y if mate else y
        return (there * SIDE + z, turn(x, step) * CORES + core)

    def spot(k, g, low_y, at_z, count):
        start = ((k * 2 + g) * 2 + core) * PART + (at_z * SIDE + low_y) * CAP
        return pl.ds(pl.multiple_of(start, CAP), count)

    def block(k, g, other, dz):
        half = 1 - half_y if other else half_y
        return rows.at[spot(k, g, 2 * half, turn(z, dz), PAIR)]

    def settle(ref, sem):
        pltpu.make_async_copy(ref, ref, sem).wait()

    def drain(ref, count, sem):
        settle(ref.at[pl.ds(0, count)], sem)

    def push(src, dst, send, recv, device):
        pltpu.make_async_remote_copy(
            src_ref=src, dst_ref=dst, send_sem=send, recv_sem=recv,
            device_id=device, device_id_type=MESH,
        ).start()

    barrier = pltpu.get_barrier_semaphore()
    partners = [sibling, across, above, below, trade]
    for step in range(SIDE):
        for mate in (False, True):
            if step or mate:
                partners.append(peer(mate, step))
    for partner in partners:
        pl.semaphore_signal(barrier, inc=1, device_id=partner, device_id_type=MESH)

    @pl.when(jnp.logical_not(guest))
    def _():
        pltpu.make_async_copy(w_in.at[0], w1, weight_recv.at[0]).start()
        pltpu.make_async_copy(w_out.at[0], w2, weight_recv.at[1]).start()

    limits = counts[...].astype(F32)
    expert_lanes = lax.broadcasted_iota(jnp.int32, (ids.shape[1], EXPERTS), 1)
    slot_lanes = lax.broadcasted_iota(jnp.int32, (ids.shape[1], EXPERTS * CAP), 1)
    picks, weighted = None, None
    ids_down, slots_down, gates_down = (
        jnp.concatenate([ref[...].astype(F32)] * 4, axis=0).T for ref in (ids, slots, gates)
    )
    for choice in range(2):
        expert = ids_down[:, choice : choice + 1].astype(jnp.int32)
        slot = slots_down[:, choice : choice + 1].astype(jnp.int32)
        limit = jnp.sum(
            jnp.where(expert == expert_lanes, limits, 0.0), axis=1, keepdims=True
        )
        place = jnp.where(slot.astype(F32) < limit, expert * CAP + slot, -1)
        pick = jnp.where(place == slot_lanes, 1.0, 0.0)
        scale = pick * gates_down[:, choice : choice + 1]
        picks = pick if picks is None else picks + pick
        weighted = scale if weighted is None else weighted + scale
    held[...] = picks.astype(BF16)
    to_slots = picks.T.astype(BF16)
    slot_gate = jnp.sum(weighted.T, axis=1, keepdims=True)
    out_x[...] = jnp.dot(to_slots, tokens[...], preferred_element_type=F32).astype(BF16)
    out_g[...] = (
        slot_gate * jnp.dot(to_slots, grad_out[...], preferred_element_type=F32)
    ).astype(BF16)
    def slots_of(expert):
        return pl.ds(pl.multiple_of(expert * CAP, CAP), CAP)

    served = x * CORES + side
    for g, source in enumerate((out_x, out_g)):
        rows[spot(0, g, y, z, CAP), :] = source[slots_of(served), :]

    pl.semaphore_wait(barrier, len(partners))

    def swap(k, mate):
        target = peer(mate, SIDE - DX[k])
        there = turn(x, SIDE - DX[k]) * CORES + (1 - side if mate else side)
        for g, source in enumerate((out_x, out_g)):
            push(
                source.at[slots_of(there)], rows.at[spot(k, g, y, z, CAP)],
                swap_send, swap_recv.at[k, int(mate)], target,
            )

    def ship(k, g, other, dz, device, event):
        where = block(k, g, other, dz)
        push(where, where, gather_send.at[k], gather_recv.at[k, event], device)

    def share(k, g, other, dz):
        where = block(k, g, other, dz)
        push(where, where, core_send.at[k], core_recv.at[k], sibling)

    def gather_first(from_y):
        for g in range(2):
            where = rows.at[spot(0, g, from_y, z, CAP)]
            for event, device in enumerate((across, above, below)):
                push(where, where, gather_send.at[0], gather_recv.at[0, event], device)
        for g in range(2):
            where = rows.at[spot(0, g, from_y, z, CAP)]
            push(where, where, core_send.at[0], core_recv.at[0], sibling)

    def gather_start(k):
        for mate in range(2):
            drain(rows, 2 * CAP, swap_recv.at[k, mate])
        for g in range(2):
            ship(k, g, False, 0, across, 0)
            ship(k, g, False, 0, above, 1)
            ship(k, g, False, 0, below, 2)
        for g in range(2):
            share(k, g, False, 0)

    def gather_mate():
        drain(rows, 2 * CAP, swap_recv.at[0, 1])
        gather_first(mate_y)

    def gather_cross(k):
        drain(rows, 2 * PAIR, gather_recv.at[k, 0])
        for g in range(2):
            ship(k, g, True, 0, above, 4)
            ship(k, g, True, 0, below, 5)
        for g in range(2):
            share(k, g, True, 0)

    def gather_pass(k):
        drain(rows, 2 * PAIR, gather_recv.at[k, 1])
        ship(k, 0, False, 3, above, 3)
        drain(rows, 2 * PAIR, gather_recv.at[k, 2])
        ship(k, 1, False, 1, below, 3)
        for g in range(2):
            share(k, g, False, 3)
            share(k, g, False, 1)

    def gather_far(k):
        drain(rows, 2 * PAIR, gather_recv.at[k, 3])
        for g in range(2):
            ship(k, g, False, 2, across, 6)
        for g in range(2):
            share(k, g, False, 2)

    def gather_end(k):
        for event, dz in ((4, 3), (5, 1), (6, 2)):
            drain(rows, 2 * PAIR, gather_recv.at[k, event])
            for g in range(2):
                share(k, g, True, dz)

    def gather_done(k):
        drain(rows, 2 * PART, core_recv.at[k])

    def section(k, g, part):
        start = ((k * 2 + g) * 2 + part) * PART
        return pl.ds(pl.multiple_of(start, PART), PART)

    def span_of(k, part):
        return pl.ds(pl.multiple_of(k * CHUNK + part * PART, PART), PART)

    def activate(k, part):
        pre = jnp.dot(rows[section(k, 0, part), :], w1[...], preferred_element_type=F32)
        activated, slope = gelu_parts(pre)
        hidden_t[:, span_of(k, part)] = activated.T.astype(BF16)
        slopes[span_of(k, part), :] = slope

    def backward(k, part):
        span = span_of(k, part)
        back_hidden = lax.dot_general(
            rows[section(k, 1, part), :], w2[...], (((1,), (1,)), ((), ())),
            preferred_element_type=F32,
        )
        change = back_hidden * slopes[span, :]
        delta[span, :] = change.astype(BF16)
        delta_t[:, span] = change.T.astype(BF16)

    def both(step, k):
        for part in range(CORES):
            step(k, part)

    def slopes_of(k, part):
        activate(k, part)
        backward(k, part)

    def to_inputs(k, part):
        span = span_of(k, part)
        for start in range(0, width, units):
            back[span, start : start + units] = lax.dot_general(
                delta[span, :], w1[start : start + units, :], (((1,), (1,)), ((), ())),
                preferred_element_type=F32,
            ).astype(BF16)

    def product(left, g, start, chunks):
        total = None
        for k in chunks:
            term = jnp.dot(
                left[:, k * CHUNK : (k + 1) * CHUNK],
                rows[pl.ds((k * 2 + g) * CHUNK, CHUNK), start : start + tile],
                preferred_element_type=F32,
            )
            total = term if total is None else total + term
        return total

    def settle_grad(ref, target, index):
        @pl.when(guest)
        def _():
            push(ref, target, grad_send.at[index], grad_recv.at[index], trade)

        @pl.when(jnp.logical_not(guest))
        def _():
            pltpu.make_async_copy(ref, target, grad_recv.at[index]).start()

    def second_weights(index):
        columns = pl.ds(index * tile, tile)
        if index:
            total = product(hidden_t, 1, index * tile, range(CHUNKS))
        else:
            total = early[...] + product(hidden_t, 1, 0, (CHUNKS - 1,))
        rounded[:, columns] = total.astype(BF16)
        settle_grad(rounded.at[:, columns], grad_second.at[:, columns], 0)

    def second_early():
        early[...] = product(hidden_t, 1, 0, range(CHUNKS - 1))

    def first_weights(index):
        span = pl.ds(index * tile, tile)
        turned[span, :] = product(delta_t, 0, index * tile, range(CHUNKS)).T.astype(BF16)
        settle_grad(turned.at[span], grad_in.at[span], 1)

    def add_start(k):
        to_inputs(k, 1 - core)
        push(
            back.at[span_of(k, 1 - core)], other_core.at[k],
            add_send.at[k], add_recv.at[k], sibling,
        )
        to_inputs(k, core)

    def lump(k, other, dz, first=0, count=PAIR):
        half = 1 - half_y if other else half_y
        start = k * CHUNK + core * PART + (turn(z, dz) * SIDE + 2 * half) * CAP + first
        return pl.ds(pl.multiple_of(start, CAP), count)

    def add(where, *terms):
        total = back[where, :].astype(F32)
        for term in terms:
            total = total + term.astype(F32)
        back[where, :] = total.astype(BF16)

    def forward(k, where, target, event, device):
        push(back.at[where], target, sum_send.at[k], sum_recv.at[k, event], device)

    def sum_start(k):
        settle(other_core.at[k], add_recv.at[k])
        add(span_of(k, core), other_core[k])
        forward(k, lump(k, True, 2), sum_a.at[k], 0, across)
        forward(k, lump(k, True, 1), sum_b.at[k, 0], 1, above)
        forward(k, lump(k, True, 3), sum_b.at[k, 1], 2, below)
        forward(k, lump(k, False, 1, CAP, CAP), sum_e.at[k, 0, pl.ds(CAP, CAP)], 6, above)
        forward(k, lump(k, False, 3, 0, CAP), sum_e.at[k, 1, pl.ds(0, CAP)], 7, below)

    def sum_far(k):
        settle(sum_a.at[k], sum_recv.at[k, 0])
        add(lump(k, False, 2), sum_a[k])
        forward(k, lump(k, False, 2, 0, CAP), sum_c.at[k, 0], 3, above)
        forward(k, lump(k, False, 2, CAP, CAP), sum_c.at[k, 1], 4, below)

    def sum_cross(k):
        settle(sum_b.at[k, 0], sum_recv.at[k, 1])
        settle(sum_b.at[k, 1], sum_recv.at[k, 2])
        add(lump(k, True, 0), sum_b[k, 0], sum_b[k, 1])
        forward(k, lump(k, True, 0), sum_d.at[k], 5, across)

    def sum_pass(k):
        settle(sum_c.at[k, 0], sum_recv.at[k, 3])
        add(lump(k, False, 1, 0, CAP), sum_c[k, 0])
        forward(k, lump(k, False, 1, 0, CAP), sum_e.at[k, 0, pl.ds(0, CAP)], 6, above)
        settle(sum_c.at[k, 1], sum_recv.at[k, 4])
        add(lump(k, False, 3, CAP, CAP), sum_c[k, 1])
        forward(k, lump(k, False, 3, CAP, CAP), sum_e.at[k, 1, pl.ds(CAP, CAP)], 7, below)

    def sum_end(k):
        settle(sum_d.at[k], sum_recv.at[k, 5])
        settle(sum_e.at[k, 0], sum_recv.at[k, 6])
        settle(sum_e.at[k, 1], sum_recv.at[k, 7])
        final[k] = (
            back[lump(k, False, 0), :].astype(F32) + sum_d[k].astype(F32)
            + sum_e[k, 0].astype(F32) + sum_e[k, 1].astype(F32)
        ).astype(BF16)
        mine = pl.ds(pl.multiple_of((y - 2 * half_y) * CAP, CAP), CAP)
        mates = pl.ds(pl.multiple_of((mate_y - 2 * half_y) * CAP, CAP), CAP)
        if k == 0:
            returned[slots_of(served), :] = final[k, mine, :]
        else:
            push(
                final.at[k, mine], returned.at[slots_of(served)],
                home_send, home_recv.at[k, 0], peer(False, DX[k]),
            )
        push(
            final.at[k, mates], returned.at[slots_of(served)],
            home_send, home_recv.at[k, 1], peer(True, DX[k]),
        )

    swap(0, True)
    gather_first(y)
    gather_mate()
    swap(1, True)
    swap(1, False)

    @pl.when(guest)
    def _():
        push(w_in.at[0], w1, weight_send.at[0], weight_recv.at[0], trade)
        push(w_out.at[0], w2, weight_send.at[1], weight_recv.at[1], trade)

    gather_pass(0)
    gather_cross(0)
    gather_start(1)
    swap(2, True)
    swap(2, False)
    gather_far(0)
    swap(3, True)
    swap(3, False)
    gather_start(2)
    gather_pass(1)
    gather_cross(1)
    gather_start(3)
    gather_far(1)
    gather_end(0)
    gather_pass(2)
    gather_cross(2)
    gather_far(2)
    gather_end(1)
    first = pltpu.make_async_copy(held, picked_out, store_sem.at[0])
    first.start()
    settle(w1, weight_recv.at[0])
    gather_done(0)
    both(activate, 0)
    gather_pass(3)
    gather_cross(3)
    gather_done(1)
    both(activate, 1)
    gather_far(3)
    gather_end(2)
    gather_done(2)
    both(activate, 2)
    second_early()
    settle(w2, weight_recv.at[1])
    both(backward, 0)
    both(backward, 1)
    both(backward, 2)
    gather_end(3)
    activate(3, core)
    gather_done(3)
    activate(3, 1 - core)
    second_weights(0)
    both(backward, 3)
    add_start(0)
    second_weights(1)
    sum_start(0)
    add_start(1)
    second_weights(2)
    sum_far(0)
    sum_cross(0)
    sum_start(1)
    add_start(2)
    second_weights(3)
    first_weights(0)
    sum_pass(0)
    sum_far(1)
    sum_cross(1)
    sum_start(2)
    add_start(3)
    first_weights(1)
    sum_end(0)
    sum_pass(1)
    sum_far(2)
    sum_cross(2)
    first_weights(2)
    sum_start(3)
    first_weights(3)
    sum_end(1)
    sum_pass(2)
    sum_far(3)
    sum_cross(3)
    sum_end(2)
    sum_pass(3)
    sum_end(3)

    for k in range(CHUNKS):
        if k:
            drain(returned, CAP, home_recv.at[k, 0])
        drain(returned, CAP, home_recv.at[k, 1])
    last = pltpu.make_async_copy(returned, returned_out, store_sem.at[1])
    last.start()
    settle(grad_second, grad_recv.at[0])
    settle(grad_in, grad_recv.at[1])

    @pl.when(guest)
    def _():
        settle(w1, weight_send.at[0])
        settle(w2, weight_send.at[1])
        settle(grad_second, grad_send.at[0])
        settle(grad_in, grad_send.at[1])

    drain(rows, 2 * (2 * SIDE - 1) * CAP, swap_send)
    drain(rows, (2 * SIDE - 1) * CAP, home_send)
    for k in range(CHUNKS):
        drain(rows, 14 * PAIR, gather_send.at[k])
        drain(rows, 2 * PART, core_send.at[k])
        drain(rows, PART, add_send.at[k])
        drain(rows, 7 * PAIR, sum_send.at[k])
    first.wait()
    last.wait()


def finish(
    picked, returned, turned, rounded,
    grad_tokens, grad_in, grad_second,
    from_first, from_second, to_first, to_second, rows, held, total, load_sem, store_sem,
):
    loads, stores = [], []
    for source, near in ((picked, held), (returned, rows)):
        loads.append(pltpu.make_async_copy(source, near, load_sem.at[len(loads)]))
    for source, near in ((turned, from_first), (rounded, from_second)):
        height = source.shape[0] // PIECES
        for piece in range(PIECES):
            span = pl.ds(piece * height, height)
            loads.append(
                pltpu.make_async_copy(source.at[span], near.at[span], load_sem.at[len(loads)])
            )
    for load in loads:
        load.start()

    def store(near, target):
        stores.append(pltpu.make_async_copy(near, target, store_sem.at[len(stores)]))
        stores[-1].start()

    for load in loads[:2]:
        load.wait()
    total[...] = jnp.dot(held[...], rows[...], preferred_element_type=F32).astype(BF16)
    store(total, grad_tokens)
    arrivals = iter(loads[2:])
    for near, wide, target in (
        (from_first, to_first, grad_in), (from_second, to_second, grad_second),
    ):
        height = near.shape[0] // PIECES
        for piece in range(PIECES):
            span = pl.ds(piece * height, height)
            next(arrivals).wait()
            wide[span, :] = near[span, :].astype(F32)
            store(wide.at[span], target.at[0, span])
    for started in stores:
        started.wait()


def body(tokens, grad_out, gate_weights, expert_ids, slot_ids, counts, w_in, w_out):
    token_rows, width = tokens.shape
    units = w_out.shape[1]
    in_vmem = pl.BlockSpec(memory_space=pltpu.VMEM)
    in_hbm = pl.BlockSpec(memory_space=pl.ANY)
    dma = pltpu.SemaphoreType.DMA
    slots = EXPERTS * CAP
    results = pl.pallas_call(
        kernel,
        out_shape=(
            jax.ShapeDtypeStruct((token_rows, slots), BF16),
            jax.ShapeDtypeStruct((slots, width), BF16),
            jax.ShapeDtypeStruct((width, units), BF16),
            jax.ShapeDtypeStruct((units, width), BF16),
        ),
        in_specs=[in_vmem] * 6 + [in_hbm] * 2,
        out_specs=(in_hbm,) * 4,
        scratch_shapes=[
            pltpu.VMEM((CHUNKS * 2 * CHUNK, width), BF16),
            pltpu.VMEM((width, units), BF16),
            pltpu.VMEM((units, width), BF16),
            pltpu.VMEM((CHUNKS * CHUNK, width), BF16),
            pltpu.VMEM((CHUNKS, PART, width), BF16),
            pltpu.VMEM((width, units), BF16),
            pltpu.VMEM((units, width), BF16),
            pltpu.VMEM((EXPERTS * CAP, width), BF16),
            pltpu.VMEM((EXPERTS * CAP, width), BF16),
            pltpu.VMEM((EXPERTS * CAP, width), BF16),
            pltpu.VMEM((token_rows, EXPERTS * CAP), BF16),
            pltpu.VMEM((units, CHUNKS * CHUNK), BF16),
            pltpu.VMEM((CHUNKS * CHUNK, units), BF16),
            pltpu.VMEM((units, CHUNKS * CHUNK), BF16),
            pltpu.VMEM((CHUNKS * CHUNK, units), F32),
            pltpu.VMEM((CHUNKS, PAIR, width), BF16),
            pltpu.VMEM((CHUNKS, 2, PAIR, width), BF16),
            pltpu.VMEM((CHUNKS, 2, CAP, width), BF16),
            pltpu.VMEM((CHUNKS, PAIR, width), BF16),
            pltpu.VMEM((CHUNKS, 2, PAIR, width), BF16),
            pltpu.VMEM((CHUNKS, PAIR, width), BF16),
            pltpu.VMEM((units, width // TILES), F32),
            dma((2,)),
            dma((2,)),
            dma((2,)),
            dma,
            dma((CHUNKS, 2)),
            dma((CHUNKS,)),
            dma((CHUNKS, 7)),
            dma((CHUNKS,)),
            dma((CHUNKS,)),
            dma((CHUNKS,)),
            dma((CHUNKS,)),
            dma((CHUNKS,)),
            dma((CHUNKS, 8)),
            dma((2,)),
            dma((2,)),
            dma,
            dma((CHUNKS, 2)),
        ],
        compiler_params=pltpu.CompilerParams(
            collective_id=0, has_side_effects=True, vmem_limit_bytes=62 * 2**20
        ),
        cost_estimate=pl.CostEstimate(
            flops=10 * NODES * EXPERTS * CAP * width * units,
            bytes_accessed=16 * width * units,
            transcendentals=0,
        ),
    )(tokens, grad_out, gate_weights.T, expert_ids.T, slot_ids.T, counts, w_in, w_out)
    return pl.pallas_call(
        finish,
        out_shape=(
            jax.ShapeDtypeStruct(tokens.shape, BF16),
            jax.ShapeDtypeStruct(w_in.shape, F32),
            jax.ShapeDtypeStruct(w_out.shape, F32),
        ),
        in_specs=[in_hbm] * 4,
        out_specs=(in_hbm,) * 3,
        scratch_shapes=[
            pltpu.VMEM((width, units), BF16),
            pltpu.VMEM((units, width), BF16),
            pltpu.VMEM((width, units), F32),
            pltpu.VMEM((units, width), F32),
            pltpu.VMEM((slots, width), BF16),
            pltpu.VMEM((token_rows, slots), BF16),
            pltpu.VMEM((token_rows, width), BF16),
            dma((2 + 2 * PIECES,)),
            dma((1 + 2 * PIECES,)),
        ],
        compiler_params=pltpu.CompilerParams(vmem_limit_bytes=62 * 2**20),
    )(*results)


def solution(mesh):
    placed = (
        P(("node", "local"), None),
        P(("node", "local"), None),
        P(("node", "local"), None),
        P(("node", "local"), None),
        P(("node", "local"), None),
        P(("node", "local"), None),
        P("local", None, "node"),
        P("local", "node", None),
    )
    return jax.shard_map(
        body,
        mesh=mesh,
        in_specs=placed,
        out_specs=(P(("node", "local"), None), P("local", None, "node"), P("local", "node", None)),
        check_vma=False,
    )
```
